512 devices in a mesh: seq: 64 (over z, x, core), chan: 8 (over y).
Axes of the slice: x: 4, y: 8, z: 8, core: 2. Of those that a mesh axis runs over, the one named last changes fastest.
Arguments:
- key_branch: bfloat16 [8192, 4096], P('seq', 'chan'), may hold values from -6 to 6
- value_branch: bfloat16 [8192, 4096], P('seq', 'chan'), may hold values from -6 to 6
- query_branch: bfloat16 [8192, 4096], P('seq', 'chan'), may hold values from -6 to 6
- long_filter: bfloat16 [8192, 4096], P('seq', 'chan'), may hold values from -1.1 to 1.1
- skip_scale: float32 [4096], P('chan'), may hold values from -1 to 1
- out_weight: bfloat16 [4096, 4096], P('chan'), may hold values from -0.125 to 0.125
Outputs:
- operator_out: bfloat16 [8192, 4096], P('seq', 'chan')
- projected: bfloat16 [8192, 4096], P('seq', 'chan')
The draws below stay inside these ranges and needn't reach their ends.
All inputs are finite; a program needn't handle non-finite values.
Results may differ from the reference program's by a relative error of at most 0.02.
Values may be sent and summed in bfloat16 or wider, within the bound.
No kernel may reach another device: no remote copies, remote signals or barrier semaphores. Data moves between devices by JAX's collectives and lax.ppermute only.
A program may use at most 64 MiB of HBM per device.

```python
import math
import jax
import jax.numpy as jnp
from jax import lax

D_OUT = 4096
TOKENS = 8192
CHANNELS = 4096


def draw_long_filter(key, part):
    key = jax.random.fold_in(key, 7)
    streams = jax.random.split(key, 8)
    positions = jnp.arange(TOKENS, dtype=jnp.float32)[:, None]
    slow_rate = jnp.exp(jax.random.uniform(streams[0], (1, CHANNELS), minval=jnp.log(0.05), maxval=jnp.log(2.0))) / TOKENS
    fast_rate = jnp.exp(jax.random.uniform(streams[1], (1, CHANNELS), minval=jnp.log(1.0 / 50.0), maxval=jnp.log(1.0 / 30.0)))
    picks = jax.random.randint(streams[2], (1, CHANNELS), 0, 100)
    breaks = jax.random.randint(streams[3], (3, CHANNELS), 0, TOKENS).astype(jnp.float32)
    drops = jax.random.uniform(streams[4], (3, CHANNELS), minval=0.5, maxval=0.8)
    echo_start = jax.random.randint(streams[6], (1, CHANNELS), TOKENS // 8, TOKENS // 2).astype(jnp.float32)
    echo_rate = jnp.exp(jax.random.uniform(streams[7], (1, CHANNELS), minval=jnp.log(0.5), maxval=jnp.log(2.0))) / TOKENS
    rates = jnp.where(picks < 50, slow_rate, fast_rate)
    noise = jnp.clip(jax.random.normal(streams[5], (TOKENS, CHANNELS)), -4.0, 4.0)
    envelope = jnp.exp(-rates * positions)
    for which_break in range(3):
        envelope = envelope * jnp.where(positions >= breaks[which_break][None, :], drops[which_break][None, :], 1.0)
    energy = jnp.expm1(-2.0 * rates * TOKENS) / jnp.expm1(-2.0 * rates)
    echo_lag = positions - echo_start
    echo_shape = jnp.where(echo_lag >= 0.0, jnp.exp(-echo_rate * jnp.maximum(echo_lag, 0.0)), 0.0)
    echo_count = TOKENS - echo_start
    echo_energy = jnp.expm1(-2.0 * echo_rate * echo_count) / jnp.expm1(-2.0 * echo_rate)
    shaped = envelope / jnp.sqrt(energy) + jnp.sqrt(0.6 / echo_energy) * echo_shape
    return jnp.clip(noise * shaped, -1.1, 1.1).astype(jnp.bfloat16)


def strengthened(drawn, stream_key, source, target, parts, factor):
    def block_of(position):
        return (jnp.arange(drawn.shape[position]) // (drawn.shape[position] // parts)).reshape((-1,) + (1,) * (drawn.ndim - 1 - position))

    first = jax.random.permutation(stream_key, parts)[block_of(target)]
    far = (block_of(target) + parts // 2) % parts
    return jnp.where((block_of(source) == first) | (block_of(source) == far), factor * drawn, drawn)


def steps_of(key, shape, pieces, low, top_value):
    loudness, own = 1.0, jax.random.fold_in(key, 6)
    for dim, blocks in pieces:
        heights = jnp.exp(jax.random.uniform(jax.random.fold_in(own, dim), (blocks,), jnp.float32, low / len(pieces), top_value / len(pieces)))
        loudness = loudness * jnp.repeat(heights, shape[dim] // blocks).reshape([-1 if axis == dim else 1 for axis in range(len(shape))])
    return loudness


def normal_values(key, shape, width, reach, shards=(), kind=jnp.bfloat16):
    result = jax.random.normal(key, shape, jnp.float32) * width
    if len(shards) > 0:
        result = steps_of(key, shape, shards, -0.22, 0.18) * result
    return jnp.clip(result, min=-reach, max=reach).astype(kind)


def bell_draw_with(key, shape, spread, most, shards, heavy, kind=jnp.bfloat16):
    values = spread * jax.random.normal(key, shape, jnp.float32)
    if shards:
        values = values * steps_of(key, shape, shards, -0.22, 0.18)
    return jnp.clip(strengthened(values, jax.random.fold_in(key, 3), *heavy), -most, most).astype(kind)


def setup_inputs(seed: int = 0) -> dict:
    key_list = jax.random.split(jax.random.key(seed), 7)
    key_branch = normal_values(key_list[0], (TOKENS, CHANNELS), 1.0, 6.0, ((0, 64), (1, 8)))
    value_branch = normal_values(key_list[1], (TOKENS, CHANNELS), 1.0, 6.0, ((0, 64), (1, 8)))
    query_branch = normal_values(key_list[2], (TOKENS, CHANNELS), 1.0, 6.0, ((0, 64), (1, 8)))
    long_filter = draw_long_filter(jax.random.fold_in(key_list[6], 71), 0)
    skip_scale = jnp.clip(jax.random.uniform(key_list[4], (CHANNELS,), jnp.float32, -1.0, 1.0) * steps_of(key_list[4], (CHANNELS,), ((0, 8),), -0.4, 0.0), -1.0, 1.0)
    out_weight = bell_draw_with(key_list[5], (CHANNELS, D_OUT), CHANNELS ** -0.5, 0.125, ((0, 8),), (0, 1, 8, 2.0))
    return {"key_branch": key_branch, "value_branch": value_branch, "query_branch": query_branch, "long_filter": long_filter, "skip_scale": skip_scale, "out_weight": out_weight}


def reference(key_branch, value_branch, query_branch, long_filter, skip_scale, out_weight):
    products = (key_branch.astype(jnp.float32) * value_branch.astype(jnp.float32)).astype(jnp.bfloat16)
    block_width = math.gcd(CHANNELS, 256)
    block_count = CHANNELS // block_width

    def convolve(members):
        signal, kernel = members
        spectrum = jnp.fft.rfft(signal, n=2 * TOKENS, axis=1) * jnp.fft.rfft(kernel, n=2 * TOKENS, axis=1)
        return jnp.fft.irfft(spectrum, n=2 * TOKENS, axis=1)[:, :TOKENS].astype(jnp.float32)

    signal_blocks = products.astype(jnp.float32).T.reshape(block_count, block_width, TOKENS)
    kernel_blocks = long_filter.astype(jnp.float32).T.reshape(block_count, block_width, TOKENS)
    convolved = lax.map(convolve, (signal_blocks, kernel_blocks)).reshape(CHANNELS, TOKENS).T
    direct = skip_scale[None, :] * products.astype(jnp.float32)
    operator_out = (query_branch.astype(jnp.float32) * (convolved + direct)).astype(jnp.bfloat16)
    projected = jnp.dot(operator_out, out_weight, preferred_element_type=jnp.float32).astype(jnp.bfloat16)
    return operator_out, projected
```

```python
import functools

import jax
import jax.numpy as jnp
import numpy as np
from jax import lax
from jax.experimental import pallas as pl
from jax.experimental.pallas import tpu as pltpu
from jax.sharding import PartitionSpec as P

f32 = jnp.float32
bf16 = jnp.bfloat16


def split(values, parts):
    pieces = []
    rest = np.asarray(values, np.float64)
    for _ in range(parts):
        piece = rest.astype(bf16)
        pieces.append(piece)
        rest = rest - piece.astype(np.float64)
    return pieces


def transform_tables(outer, inner):
    length = outer * inner
    row = np.arange(outer, dtype=np.float64)
    lane = np.arange(inner, dtype=np.float64)
    angle = 2.0 * np.pi * np.outer(row + 0.25, row) / outer
    first = np.concatenate([np.cos(angle), -np.sin(angle)], axis=0)
    twist = 2.0 * np.pi * np.outer(row + 0.25, lane) / length
    angle = 2.0 * np.pi * np.outer(lane, lane) / inner
    cos, sin = np.cos(angle), np.sin(angle)
    second = np.block([[cos, -sin], [sin, cos]])
    angle = 2.0 * np.pi * np.outer(row, row + 0.25) / outer
    last = np.concatenate([np.cos(angle), -np.sin(angle)], axis=1) / length
    first_parts = np.concatenate(split(first, 3), axis=1)
    second_parts = split(second, 2)
    back_parts = split(second.T, 2)
    last_high, last_low = split(last, 2)
    last_parts = np.concatenate([last_high, last_low, last_high], axis=1)
    return (
        first_parts,
        np.cos(twist).astype(np.float32),
        np.sin(twist).astype(np.float32),
        second_parts[0],
        second_parts[1],
        back_parts[0],
        back_parts[1],
        last_parts,
    )


def dot(a, b):
    return jnp.dot(a, b, preferred_element_type=f32)


def halves(values):
    high = values.astype(bf16)
    return high, (values - high.astype(f32)).astype(bf16)


def pack_kernel(shares, key_ref, value_ref, filter_ref, query_ref, out_ref):
    rows, chans = key_ref.shape
    group = chans // shares
    products = (key_ref[...].astype(f32) * value_ref[...].astype(f32)).astype(bf16).astype(f32)
    pieces = (products, filter_ref[...].astype(f32), query_ref[...].astype(f32))
    turned = [piece.T.reshape(shares, group, rows) for piece in pieces]
    out_ref[...] = jnp.concatenate(turned, axis=1).reshape(out_ref.shape).astype(bf16)


def convolve_kernel(
    group,
    outer,
    skip_ref,
    packed_ref,
    first_ref,
    cos_ref,
    sin_ref,
    second_high,
    second_low,
    back_high,
    back_low,
    last_ref,
    out_ref,
    wide,
    gated,
):
    inner = packed_ref.shape[1]
    signals = 2 * group
    step = 3 * group
    wide[...] = packed_ref[...].astype(f32)
    cos, sin = cos_ref[...], sin_ref[...]
    taken = [wide[pl.ds(i, outer, stride=step), :] for i in range(signals)]
    stacked = jnp.concatenate([t.astype(bf16) for t in taken], axis=1)
    front = dot(first_ref[...], jnp.concatenate([stacked] * 3, axis=0))
    rows = []
    for i in range(signals):
        re = front[:outer, i * inner : (i + 1) * inner]
        im = front[outer:, i * inner : (i + 1) * inner]
        rows.append(jnp.concatenate([re * cos + im * sin, im * cos - re * sin], axis=1))
    high, low = halves(jnp.concatenate(rows, axis=0))
    spec = dot(high, second_high[...]) + dot(low, second_high[...]) + dot(high, second_low[...])
    half = group * outer
    a_re, a_im = spec[:half, :inner], spec[:half, inner:]
    b_re, b_im = spec[half:, :inner], spec[half:, inner:]
    prod = jnp.concatenate([a_re * b_re - a_im * b_im, a_re * b_im + a_im * b_re], axis=1)
    high, low = halves(prod)
    back = dot(high, back_high[...]) + dot(low, back_high[...]) + dot(high, back_low[...])
    columns = []
    for i in range(group):
        re = back[i * outer : (i + 1) * outer, :inner]
        im = back[i * outer : (i + 1) * outer, inner:]
        columns.append(jnp.concatenate([re * cos - im * sin, re * sin + im * cos], axis=0))
    high, low = halves(jnp.concatenate(columns, axis=1))
    result = dot(last_ref[...], jnp.concatenate([high, high, low], axis=0))
    for i in range(group):
        conv = result[:, i * inner : (i + 1) * inner]
        query = wide[pl.ds(signals + i, outer, stride=step), :]
        gated[pl.ds(i, outer, stride=group), :] = query * (conv + skip_ref[i] * taken[i])
    out_ref[...] = gated[...].astype(bf16)


def project_kernel(turned_ref, weight_ref, out_ref, partial_ref):
    @pl.when(pl.program_id(0) == 0)
    def _():
        out_ref[...] = turned_ref[...].astype(f32).T.astype(bf16)

    partial_ref[0] = dot(out_ref[...], weight_ref[...]).astype(bf16)


VMEM = pl.BlockSpec(memory_space=pltpu.VMEM)
SMEM = pl.BlockSpec(memory_space=pltpu.SMEM)
params = pltpu.CompilerParams(vmem_limit_bytes=48 * 1024 * 1024)


def shards(key_branch, value_branch, query_branch, long_filter, skip_scale, out_weight):
    seq_count = lax.axis_size("seq")
    chan_count = lax.axis_size("chan")
    seq_index = lax.axis_index("seq")
    rows, chans = key_branch.shape
    group = chans // seq_count
    tables = transform_tables(seq_count, rows)
    packed = pl.pallas_call(
        functools.partial(pack_kernel, seq_count),
        out_shape=jax.ShapeDtypeStruct((3 * chans, rows), bf16),
        in_specs=[VMEM] * 4,
        out_specs=VMEM,
        compiler_params=params,
        name="pack",
    )(key_branch, value_branch, long_filter, query_branch)
    packed = lax.all_to_all(
        packed.reshape(seq_count, 3 * group, rows), "seq", split_axis=0, concat_axis=0, tiled=True
    ).reshape(3 * chans, rows)
    skip = lax.dynamic_slice(skip_scale, (seq_index * group,), (group,))
    turned = pl.pallas_call(
        functools.partial(convolve_kernel, group, seq_count),
        out_shape=jax.ShapeDtypeStruct((chans, rows), bf16),
        in_specs=[SMEM] + [VMEM] * (1 + len(tables)),
        out_specs=VMEM,
        scratch_shapes=[pltpu.VMEM((3 * chans, rows), f32), pltpu.VMEM((chans, rows), f32)],
        compiler_params=params,
        name="convolve",
    )(skip, packed, *[jnp.asarray(t) for t in tables])
    turned = lax.all_to_all(
        turned.reshape(seq_count, group, rows), "seq", split_axis=0, concat_axis=0, tiled=True
    ).reshape(chans, rows)
    width = out_weight.shape[1] // chan_count
    operator_out, partial = pl.pallas_call(
        project_kernel,
        grid=(chan_count,),
        out_shape=(
            jax.ShapeDtypeStruct((rows, chans), bf16),
            jax.ShapeDtypeStruct((chan_count, rows, width), bf16),
        ),
        in_specs=[
            pl.BlockSpec((chans, rows), lambda i: (0, 0)),
            pl.BlockSpec((chans, width), lambda i: (0, i)),
        ],
        out_specs=(
            pl.BlockSpec((rows, chans), lambda i: (0, 0)),
            pl.BlockSpec((1, rows, width), lambda i: (i, 0, 0)),
        ),
        compiler_params=params,
        name="project",
    )(turned, out_weight)
    partial = lax.all_to_all(partial, "chan", split_axis=0, concat_axis=0, tiled=True)
    projected = jnp.sum(partial.astype(f32), axis=0).astype(bf16)
    return (operator_out, projected)


def solution(mesh):
    placed = (
        P("seq", "chan"),
        P("seq", "chan"),
        P("seq", "chan"),
        P("seq", "chan"),
        P("chan"),
        P("chan", None),
    )
    return jax.shard_map(
        shards,
        mesh=mesh,
        in_specs=placed,
        out_specs=(P("seq", "chan"), P("seq", "chan")),
        check_vma=False,
    )
```

```python
import functools

import jax
import jax.numpy as jnp
import numpy as np
from jax import lax
from jax.experimental import pallas as pl
from jax.experimental.pallas import tpu as pltpu
from jax.sharding import Mesh
from jax.sharding import PartitionSpec as P

f32 = jnp.float32
bf16 = jnp.bfloat16


def split(values, parts):
    pieces = []
    rest = np.asarray(values, np.float64)
    for _ in range(parts):
        piece = rest.astype(bf16)
        pieces.append(piece)
        rest = rest - piece.astype(np.float64)
    return pieces


def transform_tables(outer, inner):
    length = outer * inner
    row = np.arange(outer, dtype=np.float64)
    lane = np.arange(inner, dtype=np.float64)
    angle = 2.0 * np.pi * np.outer(row + 0.25, row) / outer
    first = np.concatenate([np.cos(angle), -np.sin(angle)], axis=0)
    twist = 2.0 * np.pi * np.outer(row + 0.25, lane) / length
    angle = 2.0 * np.pi * np.outer(lane, lane) / inner
    cos, sin = np.cos(angle), np.sin(angle)
    second = np.block([[cos, -sin], [sin, cos]])
    angle = 2.0 * np.pi * np.outer(row, row + 0.25) / outer
    last = np.concatenate([np.cos(angle), -np.sin(angle)], axis=1) / length
    first_parts = np.concatenate(split(first, 3), axis=1)
    second_parts = split(second, 2)
    back_parts = split(second.T, 2)
    last_high, last_low = split(last, 2)
    last_parts = np.concatenate([last_high, last_low, last_high], axis=1)
    return (
        first_parts,
        np.cos(twist).astype(np.float32),
        np.sin(twist).astype(np.float32),
        second_parts[0],
        second_parts[1],
        back_parts[0],
        back_parts[1],
        last_parts,
    )


def dot(a, b):
    return jnp.dot(a, b, preferred_element_type=f32)


def halves(values):
    high = values.astype(bf16)
    return high, (values - high.astype(f32)).astype(bf16)


PAIR = 2


def served(plane, step, planes):
    return lax.rem(plane + planes + step * (PAIR * lax.rem(plane, PAIR) - 1), planes)


def place():
    plane = PAIR * lax.axis_index("quad") + lax.axis_index("side")
    return plane, plane + 1 - PAIR * lax.axis_index("side")


def columns_of(plane, width):
    return pl.ds(pl.multiple_of(plane * width, width), width)


def fetch(pairs, sems):
    copies = [pltpu.make_async_copy(src, dst, sems.at[i]) for i, (src, dst) in enumerate(pairs)]
    for copy in copies:
        copy.start()
    return copies


def wait_all(copies):
    for copy in copies:
        copy.wait()


def pack_kernel(shares, key_ref, value_ref, filter_ref, out_ref, held, sems):
    rows, chans = key_ref.shape
    group = chans // shares
    wait_all(fetch([(ref, held.at[i]) for i, ref in enumerate((key_ref, value_ref, filter_ref))], sems))
    products = (held[0].astype(f32) * held[1].astype(f32)).astype(bf16).astype(f32)
    turned = [piece.T.reshape(shares, group, rows) for piece in (products, held[2].astype(f32))]
    out_ref[...] = jnp.concatenate(turned, axis=1).reshape(out_ref.shape).astype(bf16)


def convolve_kernel(
    group,
    outer,
    skip,
    packed,
    first_ref,
    cos_ref,
    sin_ref,
    second_high,
    second_low,
    back_high,
    back_low,
    last_ref,
    out_ref,
    wide,
    turned,
):
    inner = packed.shape[1]
    signals = 2 * group
    step = 2 * group
    wide[...] = packed[...].astype(f32)
    cos, sin = cos_ref[...], sin_ref[...]
    taken = [wide[pl.ds(i, outer, stride=step), :] for i in range(signals)]
    stacked = jnp.concatenate([t.astype(bf16) for t in taken], axis=1)
    front = dot(first_ref[...], jnp.concatenate([stacked] * 3, axis=0))
    rows = []
    for i in range(signals):
        re = front[:outer, i * inner : (i + 1) * inner]
        im = front[outer:, i * inner : (i + 1) * inner]
        rows.append(jnp.concatenate([re * cos + im * sin, im * cos - re * sin], axis=1))
    high, low = halves(jnp.concatenate(rows, axis=0))
    spec = dot(high, second_high[...]) + dot(low, second_high[...]) + dot(high, second_low[...])
    half = group * outer
    a_re, a_im = spec[:half, :inner], spec[:half, inner:]
    b_re, b_im = spec[half:, :inner], spec[half:, inner:]
    prod = jnp.concatenate([a_re * b_re - a_im * b_im, a_re * b_im + a_im * b_re], axis=1)
    high, low = halves(prod)
    back = dot(high, back_high[...]) + dot(low, back_high[...]) + dot(high, back_low[...])
    columns = []
    for i in range(group):
        re = back[i * outer : (i + 1) * outer, :inner]
        im = back[i * outer : (i + 1) * outer, inner:]
        columns.append(jnp.concatenate([re * cos - im * sin, re * sin + im * cos], axis=0))
    high, low = halves(jnp.concatenate(columns, axis=1))
    result = dot(last_ref[...], jnp.concatenate([high, high, low], axis=0))
    base = (lax.axis_index("zx") * 2 + lax.axis_index("core")) * group
    for i in range(group):
        summed = result[:, i * inner : (i + 1) * inner] + skip[base + i] * taken[i]
        turned[pl.ds(i, outer, stride=group), :] = summed
    out = turned[...].astype(bf16)
    for i in range(PAIR):
        out_ref[i] = out


def ship_kernel(steps, planes, query_ref, weight_ref, packed_ref, *rest):
    del packed_ref
    *out_refs, sems = rest
    partner = place()[1]
    count, width = out_refs[0].shape
    rows = pl.ds(pl.multiple_of(lax.axis_index("core") * count, count), count)
    pairs = [(query_ref, out_refs[-1].at[pl.ds(count, query_ref.shape[0])])]
    for step, out_ref in zip(steps, out_refs, strict=True):
        columns = columns_of(served(partner, step, planes), width)
        pairs.append((weight_ref.at[rows, columns], out_ref.at[pl.ds(0, count)]))
    wait_all(fetch(pairs, sems))


def hold_kernel(*refs):
    del refs


def stage_kernel(query_ref, *rest):
    *piece_refs, weight_ref, queries_ref, sems = rest
    count = len(piece_refs) // 2
    near_refs, far_refs = piece_refs[:count], piece_refs[count:]
    core = lax.axis_index("core")
    half = weight_ref.shape[1] // 2
    near = pl.ds(pl.multiple_of(core * half, half), half)
    far = pl.ds(pl.multiple_of((1 - core) * half, half), half)
    rows = pl.ds(half, query_ref.shape[0])
    pairs = [(query_ref, queries_ref.at[0]), (near_refs[-1].at[rows], queries_ref.at[1])]
    for i in range(count):
        pairs.append((near_refs[i].at[pl.ds(0, half)], weight_ref.at[i, near]))
        pairs.append((far_refs[i].at[pl.ds(0, half)], weight_ref.at[i, far]))
    wait_all(fetch(pairs, sems))


def gate_kernel(steps, planes, turned_ref, queries_ref, other_weight, weight_ref, own_ref, *rest):
    *partial_refs, partner_ref, held, sems = rest
    plane, partner = place()
    width = held.shape[2]
    targets = [served(plane, step, planes) for step in steps] + [partner]
    copies = fetch([(weight_ref.at[:, columns_of(t, width)], held.at[i]) for i, t in enumerate(targets)], sems)
    side = lax.axis_index("side")
    other = (queries_ref[1].astype(f32) * turned_ref[1 - side].astype(f32).T).astype(bf16)
    own = (queries_ref[0].astype(f32) * turned_ref[side].astype(f32).T).astype(bf16)
    own_ref[...] = own
    across = [dot(other, other_weight[i]) for i in range(len(steps))]
    for i, partial_ref in enumerate(partial_refs):
        copies[i].wait()
        partial_ref[...] = (dot(own, held[i]) + across[i]).astype(bf16)
    copies[-1].wait()
    partner_ref[...] = dot(own, held[len(steps)]).astype(bf16)


def keep_kernel(own_ref, weight_ref, out_ref, kept_ref, held, sems):
    copies = fetch([(weight_ref.at[:, columns_of(place()[0], held.shape[1])], held)], sems)
    own = own_ref[...]
    out_ref[...] = own
    wait_all(copies)
    kept_ref[...] = dot(own, held[...])


def sum_kernel(*refs):
    *parts, out_ref = refs
    total = parts[0][...]
    for part in parts[1:]:
        total = total + part[...].astype(f32)
    out_ref[...] = total.astype(out_ref.dtype)


ANY = pl.BlockSpec(memory_space=pl.ANY)
VMEM = pl.BlockSpec(memory_space=pltpu.VMEM)
SMEM = pl.BlockSpec(memory_space=pltpu.SMEM)
params = pltpu.CompilerParams(vmem_limit_bytes=32 * 1024 * 1024)
dma = pltpu.SemaphoreType.DMA


def call(kernel, name, out_shape, in_specs, scratch=(), **options):
    options.setdefault("out_specs", [VMEM] * len(out_shape))
    return pl.pallas_call(
        kernel,
        out_shape=out_shape,
        in_specs=in_specs,
        scratch_shapes=list(scratch),
        compiler_params=params,
        name=name,
        **options,
    )


def in_vmem(*arrays):
    return [pltpu.with_memory_space_constraint(x, pltpu.VMEM) for x in arrays]


def permuted_after(arrays, after, axis, pairs):
    count = len(arrays)
    arrays = call(
        hold_kernel,
        "hold",
        [jax.ShapeDtypeStruct(x.shape, x.dtype) for x in arrays],
        [ANY] * (count + 1),
        out_specs=[ANY] * count,
        input_output_aliases={i: i for i in range(count)},
    )(*arrays, after)
    return arrays, [lax.ppermute(x, axis, pairs) for x in arrays]


def shards(key_branch, value_branch, query_branch, long_filter, skip_scale, out_weight):
    seq, chan = ("zx", "core"), ("quad", "side")
    seq_count = lax.axis_size("zx") * lax.axis_size("core")
    planes = PAIR * lax.axis_size("quad")
    steps = tuple(range(planes // PAIR - 1, 0, -1))
    rows, chans = key_branch.shape
    group = chans // seq_count
    width = out_weight.shape[1] // planes
    tables = transform_tables(seq_count, rows)
    key_branch, value_branch, query_branch, long_filter, out_weight = [
        pltpu.with_memory_space_constraint(x, pltpu.HBM)
        for x in (key_branch, value_branch, query_branch, long_filter, out_weight)
    ]
    (packed,) = call(
        functools.partial(pack_kernel, seq_count),
        "pack",
        [pltpu.VMEM((2 * chans, rows), bf16)],
        [ANY] * 3,
        [pltpu.VMEM((3, rows, chans), bf16), dma((3,))],
    )(key_branch, value_branch, long_filter)
    arrived = lax.all_to_all(
        packed.reshape(seq_count, 2 * group, rows), seq, split_axis=0, concat_axis=0, tiled=True
    ).reshape(2 * chans, rows)
    swap = [(0, 1), (1, 0)]
    half = chans // 2
    piece_rows = [half] * (len(steps) - 1) + [half + rows]
    near = call(
        functools.partial(ship_kernel, steps, planes),
        "ship",
        [pltpu.VMEM((count, width), bf16) for count in piece_rows],
        [ANY] * 3,
        [dma((1 + len(steps),))],
    )(query_branch, out_weight, packed)
    near = [lax.ppermute(x, "side", swap) for x in near]
    (turned,) = call(
        functools.partial(convolve_kernel, group, seq_count),
        "convolve",
        [pltpu.VMEM((PAIR, chans, rows), bf16)],
        [SMEM] + [VMEM] * (1 + len(tables)),
        [pltpu.VMEM((2 * chans, rows), f32), pltpu.VMEM((chans, rows), f32)],
    )(skip_scale, arrived, *[jnp.asarray(t) for t in tables])
    near, far = permuted_after(near, turned, "core", swap)
    staged = call(
        stage_kernel,
        "stage",
        [pltpu.VMEM((len(steps), chans, width), bf16), pltpu.VMEM((PAIR, rows, chans), bf16)],
        [ANY] * (1 + 2 * len(steps)),
        [dma((2 * len(steps) + 2,))],
    )(query_branch, *near, *far)
    other_weight, queries = in_vmem(*staged)
    turned = lax.all_to_all(
        turned.reshape(PAIR * seq_count, group, rows), ("side",) + seq, split_axis=0, concat_axis=0, tiled=True
    ).reshape(PAIR, chans, rows)
    block = pltpu.VMEM((rows, width), bf16)
    own, *sent, partner = call(
        functools.partial(gate_kernel, steps, planes),
        "gate",
        [pltpu.VMEM((rows, chans), bf16)] + [block] * (len(steps) + 1),
        [VMEM] * 3 + [ANY],
        [pltpu.VMEM((len(steps) + 1, chans, width), bf16), dma((len(steps) + 1,))],
    )(turned, queries, other_weight, out_weight)
    operator_out, kept = call(
        keep_kernel,
        "keep",
        [jax.ShapeDtypeStruct((rows, chans), bf16), pltpu.VMEM((rows, width), f32)],
        [VMEM, ANY],
        [pltpu.VMEM((chans, width), bf16), dma((1,))],
    )(own, out_weight)
    parts = [kept]
    for part, step in zip(sent, steps, strict=True):
        pairs = [(i, (i + (step if i % PAIR else planes - step)) % planes) for i in range(planes)]
        parts.append(lax.ppermute(part, chan, pairs))
    parts.append(lax.ppermute(partner, "side", swap))
    (projected,) = call(sum_kernel, "sum", [jax.ShapeDtypeStruct((rows, width), bf16)], [VMEM] * len(parts))(*parts)
    return (operator_out, projected)


def solution(mesh):
    seq_count, chan_count = mesh.shape["seq"], mesh.shape["chan"]
    shape = (seq_count // 2, 2, chan_count // PAIR, PAIR)
    paired = Mesh(mesh.devices.reshape(shape), ("zx", "core", "quad", "side"))
    seq, chan = ("zx", "core"), ("quad", "side")
    placed = (
        P(seq, chan),
        P(seq, chan),
        P(seq, chan),
        P(seq, chan),
        P(chan),
        P(chan, None),
    )
    return jax.shard_map(
        shards,
        mesh=paired,
        in_specs=placed,
        out_specs=(P(seq, chan), P(seq, chan)),
        check_vma=False,
    )
```

```python
import functools

import jax
import jax.numpy as jnp
import numpy as np
from jax import lax
from jax.experimental import pallas as pl
from jax.experimental.pallas import tpu as pltpu
from jax.sharding import Mesh
from jax.sharding import PartitionSpec as P

f32 = jnp.float32
bf16 = jnp.bfloat16


def split(values, parts):
    pieces = []
    rest = np.asarray(values, np.float64)
    for _ in range(parts):
        piece = rest.astype(bf16)
        pieces.append(piece)
        rest = rest - piece.astype(np.float64)
    return pieces


def transform_tables(outer, inner):
    length = outer * inner
    row = np.arange(outer, dtype=np.float64)
    lane = np.arange(inner, dtype=np.float64)
    angle = 2.0 * np.pi * np.outer(row + 0.25, row) / outer
    first = np.concatenate([np.cos(angle), -np.sin(angle)], axis=0)
    twist = 2.0 * np.pi * np.outer(row + 0.25, lane) / length
    angle = 2.0 * np.pi * np.outer(lane, lane) / inner
    cos, sin = np.cos(angle), np.sin(angle)
    second = np.block([[cos, -sin], [sin, cos]])
    angle = 2.0 * np.pi * np.outer(row, row + 0.25) / outer
    last = np.concatenate([np.cos(angle), -np.sin(angle)], axis=1) / length
    first_parts = np.concatenate(split(first, 3), axis=1)
    second_parts = split(second, 2)
    back_parts = split(second.T, 2)
    last_high, last_low = split(last, 2)
    last_parts = np.concatenate([last_high, last_low, last_high], axis=1)
    return (
        first_parts,
        np.cos(twist).astype(np.float32),
        np.sin(twist).astype(np.float32),
        second_parts[0],
        second_parts[1],
        back_parts[0],
        back_parts[1],
        last_parts,
    )


def dot(a, b):
    return jnp.dot(a, b, preferred_element_type=f32)


def halves(values):
    high = values.astype(bf16)
    return high, (values - high.astype(f32)).astype(bf16)


PAIR = 2


def served(plane, step, planes):
    return lax.rem(plane + planes + step * (PAIR * lax.rem(plane, PAIR) - 1), planes)


def place():
    plane = PAIR * lax.axis_index("quad") + lax.axis_index("side")
    return plane, plane + 1 - PAIR * lax.axis_index("side")


def columns_of(plane, width):
    return pl.ds(pl.multiple_of(plane * width, width), width)


def fetch(pairs, sems):
    copies = [pltpu.make_async_copy(src, dst, sems.at[i]) for i, (src, dst) in enumerate(pairs)]
    for copy in copies:
        copy.start()
    return copies


def wait_all(copies):
    for copy in copies:
        copy.wait()


def pack_kernel(shares, key_ref, value_ref, filter_ref, out_ref, held, sems):
    rows, chans = key_ref.shape
    group = chans // shares
    wait_all(fetch([(ref, held.at[i]) for i, ref in enumerate((key_ref, value_ref, filter_ref))], sems))
    products = (held[0].astype(f32) * held[1].astype(f32)).astype(bf16).astype(f32)
    turned = [piece.T.reshape(shares, group, rows) for piece in (products, held[2].astype(f32))]
    out_ref[...] = jnp.concatenate(turned, axis=1).reshape(out_ref.shape).astype(bf16)


def convolve_kernel(
    group,
    outer,
    skip,
    packed,
    first_ref,
    cos_ref,
    sin_ref,
    second_high,
    second_low,
    back_high,
    back_low,
    last_ref,
    out_ref,
    wide,
    turned,
):
    inner = packed.shape[1]
    signals = 2 * group
    step = 2 * group
    wide[...] = packed[...].astype(f32)
    cos, sin = cos_ref[...], sin_ref[...]
    taken = [wide[pl.ds(i, outer, stride=step), :] for i in range(signals)]
    stacked = jnp.concatenate([t.astype(bf16) for t in taken], axis=1)
    front = dot(first_ref[...], jnp.concatenate([stacked] * 3, axis=0))
    rows = []
    for i in range(signals):
        re = front[:outer, i * inner : (i + 1) * inner]
        im = front[outer:, i * inner : (i + 1) * inner]
        rows.append(jnp.concatenate([re * cos + im * sin, im * cos - re * sin], axis=1))
    high, low = halves(jnp.concatenate(rows, axis=0))
    spec = dot(high, second_high[...]) + dot(low, second_high[...]) + dot(high, second_low[...])
    half = group * outer
    a_re, a_im = spec[:half, :inner], spec[:half, inner:]
    b_re, b_im = spec[half:, :inner], spec[half:, inner:]
    prod = jnp.concatenate([a_re * b_re - a_im * b_im, a_re * b_im + a_im * b_re], axis=1)
    high, low = halves(prod)
    back = dot(high, back_high[...]) + dot(low, back_high[...]) + dot(high, back_low[...])
    columns = []
    for i in range(group):
        re = back[i * outer : (i + 1) * outer, :inner]
        im = back[i * outer : (i + 1) * outer, inner:]
        columns.append(jnp.concatenate([re * cos - im * sin, re * sin + im * cos], axis=0))
    high, low = halves(jnp.concatenate(columns, axis=1))
    result = dot(last_ref[...], jnp.concatenate([high, high, low], axis=0))
    base = (lax.axis_index("zx") * 2 + lax.axis_index("core")) * group
    for i in range(group):
        summed = result[:, i * inner : (i + 1) * inner] + skip[base + i] * taken[i]
        turned[pl.ds(i, outer, stride=group), :] = summed
    out = turned[...].astype(bf16)
    for i in range(PAIR):
        out_ref[i] = out


def segments(steps, half, rows):
    middle = len(steps) // 2
    found, at = [], [0, 0]

    def put(piece, index, row, count):
        found.append((piece, at[piece], index, row, count))
        at[piece] += count

    for index in range(middle):
        put(0, index, 0, half)
    put(0, middle, 0, half // 2)
    put(1, middle, half // 2, half // 2)
    for index in range(middle + 1, len(steps)):
        put(1, index, 0, half)
    for piece in range(2):
        put(piece, len(steps), piece * rows // 2, rows // 2)
    return at[0], found


def ship_kernel(steps, planes, found, query_ref, weight_ref, packed_ref, *rest):
    del packed_ref
    *out_refs, sems = rest
    partner = place()[1]
    width = out_refs[0].shape[1]
    base = lax.axis_index("core") * (weight_ref.shape[0] // 2)
    pairs = []
    for piece, at, index, row, count in found:
        if index < len(steps):
            rows = pl.ds(pl.multiple_of(base + row, 16), count)
            source = weight_ref.at[rows, columns_of(served(partner, steps[index], planes), width)]
        else:
            source = query_ref.at[pl.ds(row, count)]
        pairs.append((source, out_refs[piece].at[pl.ds(at, count)]))
    wait_all(fetch(pairs, sems))


def hold_kernel(*refs):
    del refs


def stage_kernel(steps, planes, query_ref, weight_ref, after_ref, early_ref, query_out, late_ref, sems):
    del after_ref
    plane, partner = place()
    width = early_ref.shape[2]
    early = early_ref.shape[0]
    targets = [served(plane, step, planes) for step in steps] + [partner]
    pairs = [(query_ref, query_out)]
    for i, target in enumerate(targets):
        held = early_ref.at[i] if i < early else late_ref.at[i - early]
        pairs.append((weight_ref.at[:, columns_of(target, width)], held))
    wait_all(fetch(pairs, sems))


def across(found, index, other, near_refs, far_refs):
    half = other.shape[1] // 2
    low, high = other[:, :half], other[:, half:]
    first = lax.axis_index("core") == 0
    near, far = jnp.where(first, low, high), jnp.where(first, high, low)
    total = None
    for piece, at, owner, row, count in found:
        if owner == index:
            rows = pl.ds(at, count)
            part = dot(near[:, row : row + count], near_refs[piece][rows, :])
            part = part + dot(far[:, row : row + count], far_refs[piece][rows, :])
            total = part if total is None else total + part
    return total


def gate_kernel(found, turned_ref, query_ref, early_ref, *rest):
    near_refs, far_refs, (own_ref, other_ref, *partial_refs) = rest[:2], rest[2:4], rest[4:]
    side = lax.axis_index("side")
    count = max(index for _, _, index, _, _ in found)
    passed = [near_refs[piece][pl.ds(at, size), :] for piece, at, index, _, size in found if index == count]
    passed = jnp.concatenate(passed, axis=0)
    other = (passed.astype(f32) * turned_ref[1 - side].astype(f32).T).astype(bf16)
    own = (query_ref[...].astype(f32) * turned_ref[side].astype(f32).T).astype(bf16)
    own_ref[...] = own
    other_ref[...] = other
    for i, partial_ref in enumerate(partial_refs):
        partial_ref[...] = (dot(own, early_ref[i]) + across(found, i, other, near_refs, far_refs)).astype(bf16)


def near_kernel(found, index, own_ref, other_ref, late_ref, *rest):
    near_refs, far_refs, (served_ref, partner_ref) = rest[:2], rest[2:4], rest[4:]
    own = own_ref[...]
    served_ref[...] = (dot(own, late_ref[0]) + across(found, index, other_ref[...], near_refs, far_refs)).astype(bf16)
    partner_ref[...] = dot(own, late_ref[1]).astype(bf16)


def keep_kernel(own_ref, weight_ref, out_ref, kept_ref, held, sems):
    copies = fetch([(weight_ref.at[:, columns_of(place()[0], held.shape[1])], held)], sems)
    own = own_ref[...]
    out_ref[...] = own
    wait_all(copies)
    kept_ref[...] = dot(own, held[...])


def sum_kernel(*refs):
    *parts, out_ref = refs
    total = parts[0][...]
    for part in parts[1:]:
        total = total + part[...].astype(f32)
    out_ref[...] = total.astype(out_ref.dtype)


ANY = pl.BlockSpec(memory_space=pl.ANY)
VMEM = pl.BlockSpec(memory_space=pltpu.VMEM)
SMEM = pl.BlockSpec(memory_space=pltpu.SMEM)
params = pltpu.CompilerParams(vmem_limit_bytes=32 * 1024 * 1024)
dma = pltpu.SemaphoreType.DMA


def call(kernel, name, out_shape, in_specs, scratch=(), **options):
    options.setdefault("out_specs", [VMEM] * len(out_shape))
    return pl.pallas_call(
        kernel,
        out_shape=out_shape,
        in_specs=in_specs,
        scratch_shapes=list(scratch),
        compiler_params=params,
        name=name,
        **options,
    )


def in_vmem(*arrays):
    return [pltpu.with_memory_space_constraint(x, pltpu.VMEM) for x in arrays]


def permuted_after(array, after, axis, pairs):
    (array,) = call(
        hold_kernel,
        "hold",
        [jax.ShapeDtypeStruct(array.shape, array.dtype)],
        [ANY] * 2,
        out_specs=[ANY],
        input_output_aliases={0: 0},
    )(array, after)
    return array, lax.ppermute(array, axis, pairs)


def shards(key_branch, value_branch, query_branch, long_filter, skip_scale, out_weight):
    seq, chan = ("zx", "core"), ("quad", "side")
    seq_count = lax.axis_size("zx") * lax.axis_size("core")
    planes = PAIR * lax.axis_size("quad")
    steps = tuple(range(planes // PAIR - 1, 0, -1))
    rows, chans = key_branch.shape
    group = chans // seq_count
    width = out_weight.shape[1] // planes
    tables = transform_tables(seq_count, rows)
    key_branch, value_branch, query_branch, long_filter, out_weight = [
        pltpu.with_memory_space_constraint(x, pltpu.HBM)
        for x in (key_branch, value_branch, query_branch, long_filter, out_weight)
    ]
    (packed,) = call(
        functools.partial(pack_kernel, seq_count),
        "pack",
        [pltpu.VMEM((2 * chans, rows), bf16)],
        [ANY] * 3,
        [pltpu.VMEM((3, rows, chans), bf16), dma((3,))],
    )(key_branch, value_branch, long_filter)
    arrived = lax.all_to_all(
        packed.reshape(seq_count, 2 * group, rows), seq, split_axis=0, concat_axis=0, tiled=True
    ).reshape(2 * chans, rows)
    swap = [(0, 1), (1, 0)]
    size, found = segments(steps, chans // 2, rows)
    near = call(
        functools.partial(ship_kernel, steps, planes, found),
        "ship",
        [pltpu.VMEM((size, width), bf16)] * 2,
        [ANY] * 3,
        [dma((len(found),))],
    )(query_branch, out_weight, packed)
    near = [lax.ppermute(x, "side", swap) for x in near]
    (turned,) = call(
        functools.partial(convolve_kernel, group, seq_count),
        "convolve",
        [pltpu.VMEM((PAIR, chans, rows), bf16)],
        [SMEM] + [VMEM] * (1 + len(tables)),
        [pltpu.VMEM((2 * chans, rows), f32), pltpu.VMEM((chans, rows), f32)],
    )(skip_scale, arrived, *[jnp.asarray(t) for t in tables])
    near, far = zip(*[permuted_after(x, turned, "core", swap) for x in near], strict=True)
    early = len(steps) - 1
    early_weight, query, late_weight = call(
        functools.partial(stage_kernel, steps, planes),
        "stage",
        [
            pltpu.VMEM((early, chans, width), bf16),
            pltpu.VMEM((rows, chans), bf16),
            pltpu.HBM((2, chans, width), bf16),
        ],
        [ANY] * 3,
        [dma((len(steps) + 2,))],
    )(query_branch, out_weight, turned)
    early_weight, query = in_vmem(early_weight, query)
    pieces = in_vmem(*near, *far)
    turned = lax.all_to_all(
        turned.reshape(PAIR * seq_count, group, rows), ("side",) + seq, split_axis=0, concat_axis=0, tiled=True
    ).reshape(PAIR, chans, rows)
    block = pltpu.VMEM((rows, width), bf16)
    gated = pltpu.VMEM((rows, chans), bf16)
    own, other, *sent = call(
        functools.partial(gate_kernel, found),
        "gate",
        [gated] * 2 + [block] * early,
        [VMEM] * 7,
        cost_estimate=pl.CostEstimate(flops=4 * 10**9, bytes_accessed=16 * 2**20, transcendentals=0),
    )(turned, query, early_weight, *pieces)
    last, partner = call(
        functools.partial(near_kernel, found, early), "near", [block] * 2, [VMEM] * 7
    )(own, other, late_weight, *pieces)
    operator_out, kept = call(
        keep_kernel,
        "keep",
        [jax.ShapeDtypeStruct((rows, chans), bf16), pltpu.VMEM((rows, width), f32)],
        [VMEM, ANY],
        [pltpu.VMEM((chans, width), bf16), dma((1,))],
    )(own, out_weight)
    parts = [kept]
    for part, step in zip((*sent, last), steps, strict=True):
        pairs = [(i, (i + (step if i % PAIR else planes - step)) % planes) for i in range(planes)]
        parts.append(lax.ppermute(part, chan, pairs))
    parts.append(lax.ppermute(partner, "side", swap))
    (projected,) = call(sum_kernel, "sum", [jax.ShapeDtypeStruct((rows, width), bf16)], [VMEM] * len(parts))(*parts)
    return (operator_out, projected)


def solution(mesh):
    seq_count, chan_count = mesh.shape["seq"], mesh.shape["chan"]
    shape = (seq_count // 2, 2, chan_count // PAIR, PAIR)
    paired = Mesh(mesh.devices.reshape(shape), ("zx", "core", "quad", "side"))
    seq, chan = ("zx", "core"), ("quad", "side")
    placed = (
        P(seq, chan),
        P(seq, chan),
        P(seq, chan),
        P(seq, chan),
        P(chan),
        P(chan, None),
    )
    return jax.shard_map(
        shards,
        mesh=paired,
        in_specs=placed,
        out_specs=(P(seq, chan), P(seq, chan)),
        check_vma=False,
    )
```

```python
import functools

import jax
import jax.numpy as jnp
import numpy as np
from jax import lax
from jax.experimental import pallas as pl
from jax.experimental.pallas import tpu as pltpu
from jax.sharding import Mesh
from jax.sharding import PartitionSpec as P

f32 = jnp.float32
bf16 = jnp.bfloat16


def split(values, parts):
    pieces = []
    rest = np.asarray(values, np.float64)
    for _ in range(parts):
        piece = rest.astype(bf16)
        pieces.append(piece)
        rest = rest - piece.astype(np.float64)
    return pieces


def transform_tables(outer, inner):
    length = outer * inner
    row = np.arange(outer, dtype=np.float64)
    lane = np.arange(inner, dtype=np.float64)
    angle = 2.0 * np.pi * np.outer(row + 0.25, row) / outer
    first = np.concatenate([np.cos(angle), -np.sin(angle)], axis=0)
    twist = 2.0 * np.pi * np.outer(row + 0.25, lane) / length
    angle = 2.0 * np.pi * np.outer(lane, lane) / inner
    cos, sin = np.cos(angle), np.sin(angle)
    second = np.block([[cos, -sin], [sin, cos]])
    angle = 2.0 * np.pi * np.outer(row, row + 0.25) / outer
    last = np.concatenate([np.cos(angle), -np.sin(angle)], axis=1) / length
    first_parts = np.concatenate(split(first, 3), axis=1)
    second_parts = split(second, 2)
    back_parts = split(second.T, 2)
    last_high, last_low = split(last, 2)
    last_parts = np.concatenate([last_high, last_low, last_high], axis=1)
    return (
        first_parts,
        np.cos(twist).astype(np.float32),
        np.sin(twist).astype(np.float32),
        second_parts[0],
        second_parts[1],
        back_parts[0],
        back_parts[1],
        last_parts,
    )


def dot(a, b):
    return jnp.dot(a, b, preferred_element_type=f32)


def halves(values):
    high = values.astype(bf16)
    return high, (values - high.astype(f32)).astype(bf16)


PAIR = 2


def served(plane, step, planes):
    return lax.rem(plane + planes + step * (PAIR * lax.rem(plane, PAIR) - 1), planes)


def place():
    plane = PAIR * lax.axis_index("quad") + lax.axis_index("side")
    return plane, plane + 1 - PAIR * lax.axis_index("side")


def columns_of(plane, width):
    return pl.ds(pl.multiple_of(plane * width, width), width)


def fetch(pairs, sems):
    copies = [pltpu.make_async_copy(src, dst, sems.at[i]) for i, (src, dst) in enumerate(pairs)]
    for copy in copies:
        copy.start()
    return copies


def wait_all(copies):
    for copy in copies:
        copy.wait()


def pack_kernel(shares, key_ref, value_ref, filter_ref, out_ref, held, sems):
    rows, chans = key_ref.shape
    group = chans // shares
    wait_all(fetch([(ref, held.at[i]) for i, ref in enumerate((key_ref, value_ref, filter_ref))], sems))
    products = (held[0].astype(f32) * held[1].astype(f32)).astype(bf16).astype(f32)
    turned = [piece.T.reshape(shares, group, rows) for piece in (products, held[2].astype(f32))]
    out_ref[...] = jnp.concatenate(turned, axis=1).reshape(out_ref.shape).astype(bf16)


def convolve_kernel(
    group,
    outer,
    skip,
    packed,
    first_ref,
    cos_ref,
    sin_ref,
    second_high,
    second_low,
    back_high,
    back_low,
    last_ref,
    out_ref,
    wide,
    turned,
):
    inner = packed.shape[1]
    signals = 2 * group
    step = 2 * group
    wide[...] = packed[...].astype(f32)
    cos, sin = cos_ref[...], sin_ref[...]
    taken = [wide[pl.ds(i, outer, stride=step), :] for i in range(signals)]
    stacked = jnp.concatenate([t.astype(bf16) for t in taken], axis=1)
    front = dot(first_ref[...], jnp.concatenate([stacked] * 3, axis=0))
    rows = []
    for i in range(signals):
        re = front[:outer, i * inner : (i + 1) * inner]
        im = front[outer:, i * inner : (i + 1) * inner]
        rows.append(jnp.concatenate([re * cos + im * sin, im * cos - re * sin], axis=1))
    high, low = halves(jnp.concatenate(rows, axis=0))
    spec = dot(high, second_high[...]) + dot(low, second_high[...]) + dot(high, second_low[...])
    half = group * outer
    a_re, a_im = spec[:half, :inner], spec[:half, inner:]
    b_re, b_im = spec[half:, :inner], spec[half:, inner:]
    prod = jnp.concatenate([a_re * b_re - a_im * b_im, a_re * b_im + a_im * b_re], axis=1)
    high, low = halves(prod)
    back = dot(high, back_high[...]) + dot(low, back_high[...]) + dot(high, back_low[...])
    columns = []
    for i in range(group):
        re = back[i * outer : (i + 1) * outer, :inner]
        im = back[i * outer : (i + 1) * outer, inner:]
        columns.append(jnp.concatenate([re * cos - im * sin, re * sin + im * cos], axis=0))
    high, low = halves(jnp.concatenate(columns, axis=1))
    result = dot(last_ref[...], jnp.concatenate([high, high, low], axis=0))
    base = (lax.axis_index("zx") * 2 + lax.axis_index("core")) * group
    for i in range(group):
        summed = result[:, i * inner : (i + 1) * inner] + skip[base + i] * taken[i]
        turned[pl.ds(i, outer, stride=group), :] = summed
    out = turned[...].astype(bf16)
    for i in range(PAIR):
        out_ref[i] = out


def segments(steps, half, rows):
    middle = len(steps) // 2
    found, at = [], [0, 0]

    def put(piece, index, row, count):
        found.append((piece, at[piece], index, row, count))
        at[piece] += count

    for index in range(middle):
        put(0, index, 0, half)
    put(0, middle, 0, half // 2)
    put(1, middle, half // 2, half // 2)
    for index in range(middle + 1, len(steps)):
        put(1, index, 0, half)
    for piece in range(2):
        put(piece, len(steps), piece * rows // 2, rows // 2)
    return at[0], found


def ship_kernel(steps, planes, found, query_ref, weight_ref, packed_ref, *rest):
    del packed_ref
    *out_refs, sems = rest
    partner = place()[1]
    width = out_refs[0].shape[1]
    base = lax.axis_index("core") * (weight_ref.shape[0] // 2)
    pairs = []
    for piece, at, index, row, count in found:
        if index < len(steps):
            rows = pl.ds(pl.multiple_of(base + row, 16), count)
            source = weight_ref.at[rows, columns_of(served(partner, steps[index], planes), width)]
        else:
            source = query_ref.at[pl.ds(row, count)]
        pairs.append((source, out_refs[piece].at[pl.ds(at, count)]))
    wait_all(fetch(pairs, sems))


def hold_kernel(*refs):
    del refs


def stage_kernel(steps, planes, query_ref, weight_ref, after_ref, early_ref, query_out, late_ref, sems):
    del after_ref
    plane, partner = place()
    width = early_ref.shape[2]
    early = early_ref.shape[0]
    targets = [served(plane, step, planes) for step in steps] + [partner]
    pairs = [(query_ref, query_out)]
    for i, target in enumerate(targets):
        held = early_ref.at[i] if i < early else late_ref.at[i - early]
        pairs.append((weight_ref.at[:, columns_of(target, width)], held))
    wait_all(fetch(pairs, sems))


def across(found, index, other, near_refs, far_refs):
    half = other.shape[1] // 2
    low, high = other[:, :half], other[:, half:]
    first = lax.axis_index("core") == 0
    near, far = jnp.where(first, low, high), jnp.where(first, high, low)
    total = None
    for piece, at, owner, row, count in found:
        if owner == index:
            rows = pl.ds(at, count)
            part = dot(near[:, row : row + count], near_refs[piece][rows, :])
            part = part + dot(far[:, row : row + count], far_refs[piece][rows, :])
            total = part if total is None else total + part
    return total


def gate_kernel(found, turned_ref, query_ref, early_ref, *rest):
    near_refs, far_refs, (own_ref, other_ref, *partial_refs) = rest[:2], rest[2:4], rest[4:]
    side = lax.axis_index("side")
    count = max(index for _, _, index, _, _ in found)
    passed = [near_refs[piece][pl.ds(at, size), :] for piece, at, index, _, size in found if index == count]
    passed = jnp.concatenate(passed, axis=0)
    other = (passed.astype(f32) * turned_ref[1 - side].astype(f32).T).astype(bf16)
    own = (query_ref[...].astype(f32) * turned_ref[side].astype(f32).T).astype(bf16)
    own_ref[...] = own
    other_ref[...] = other
    for i, partial_ref in enumerate(partial_refs):
        partial_ref[...] = (dot(own, early_ref[i]) + across(found, i, other, near_refs, far_refs)).astype(bf16)


def near_kernel(found, index, own_ref, other_ref, late_ref, *rest):
    near_refs, far_refs, (served_ref, partner_ref) = rest[:2], rest[2:4], rest[4:]
    own = own_ref[...]
    served_ref[...] = (dot(own, late_ref[0]) + across(found, index, other_ref[...], near_refs, far_refs)).astype(bf16)
    partner_ref[...] = dot(own, late_ref[1]).astype(bf16)


def keep_kernel(own_ref, weight_ref, out_ref, kept_ref, held, sems):
    copies = fetch([(weight_ref.at[:, columns_of(place()[0], held.shape[1])], held)], sems)
    own = own_ref[...]
    out_ref[...] = own
    wait_all(copies)
    kept_ref[...] = dot(own, held[...])


def sum_kernel(*refs):
    *parts, out_ref = refs
    total = parts[0][...]
    for part in parts[1:]:
        total = total + part[...].astype(f32)
    out_ref[...] = total.astype(out_ref.dtype)


ANY = pl.BlockSpec(memory_space=pl.ANY)
VMEM = pl.BlockSpec(memory_space=pltpu.VMEM)
SMEM = pl.BlockSpec(memory_space=pltpu.SMEM)
params = pltpu.CompilerParams(vmem_limit_bytes=32 * 1024 * 1024)
dma = pltpu.SemaphoreType.DMA


def call(kernel, name, out_shape, in_specs, scratch=(), **options):
    options.setdefault("out_specs", [VMEM] * len(out_shape))
    return pl.pallas_call(
        kernel,
        out_shape=out_shape,
        in_specs=in_specs,
        scratch_shapes=list(scratch),
        compiler_params=params,
        name=name,
        **options,
    )


def in_vmem(*arrays):
    return [pltpu.with_memory_space_constraint(x, pltpu.VMEM) for x in arrays]


def permuted_after(array, after, axis, pairs):
    (array,) = call(
        hold_kernel,
        "hold",
        [jax.ShapeDtypeStruct(array.shape, array.dtype)],
        [ANY] * 2,
        out_specs=[ANY],
        input_output_aliases={0: 0},
    )(array, after)
    return array, lax.ppermute(array, axis, pairs)


def shards(key_branch, value_branch, query_branch, long_filter, skip_scale, out_weight):
    seq, chan = ("zx", "core"), ("quad", "side")
    seq_count = lax.axis_size("zx") * lax.axis_size("core")
    planes = PAIR * lax.axis_size("quad")
    steps = (2, 3, 1)
    assert planes == PAIR * (len(steps) + 1)
    rows, chans = key_branch.shape
    group = chans // seq_count
    width = out_weight.shape[1] // planes
    tables = transform_tables(seq_count, rows)
    key_branch, value_branch, query_branch, long_filter, out_weight = [
        pltpu.with_memory_space_constraint(x, pltpu.HBM)
        for x in (key_branch, value_branch, query_branch, long_filter, out_weight)
    ]
    (packed,) = call(
        functools.partial(pack_kernel, seq_count),
        "pack",
        [pltpu.VMEM((2 * chans, rows), bf16)],
        [ANY] * 3,
        [pltpu.VMEM((3, rows, chans), bf16), dma((3,))],
    )(key_branch, value_branch, long_filter)
    arrived = lax.all_to_all(
        packed.reshape(seq_count, 2 * group, rows), seq, split_axis=0, concat_axis=0, tiled=True
    ).reshape(2 * chans, rows)
    swap = [(0, 1), (1, 0)]
    size, found = segments(steps, chans // 2, rows)
    near = call(
        functools.partial(ship_kernel, steps, planes, found),
        "ship",
        [pltpu.VMEM((size, width), bf16)] * 2,
        [ANY] * 3,
        [dma((len(found),))],
    )(query_branch, out_weight, packed)
    near = [lax.ppermute(x, "side", swap) for x in near]
    (turned,) = call(
        functools.partial(convolve_kernel, group, seq_count),
        "convolve",
        [pltpu.VMEM((PAIR, chans, rows), bf16)],
        [SMEM] + [VMEM] * (1 + len(tables)),
        [pltpu.VMEM((2 * chans, rows), f32), pltpu.VMEM((chans, rows), f32)],
    )(skip_scale, arrived, *[jnp.asarray(t) for t in tables])
    near, far = zip(*[permuted_after(x, turned, "core", swap) for x in near], strict=True)
    early = len(steps) - 1
    early_weight, query, late_weight = call(
        functools.partial(stage_kernel, steps, planes),
        "stage",
        [
            pltpu.VMEM((early, chans, width), bf16),
            pltpu.VMEM((rows, chans), bf16),
            pltpu.HBM((2, chans, width), bf16),
        ],
        [ANY] * 3,
        [dma((len(steps) + 2,))],
    )(query_branch, out_weight, turned)
    early_weight, query = in_vmem(early_weight, query)
    pieces = in_vmem(*near, *far)
    turned = lax.all_to_all(
        turned.reshape(PAIR * seq_count, group, rows), ("side",) + seq, split_axis=0, concat_axis=0, tiled=True
    ).reshape(PAIR, chans, rows)
    block = pltpu.VMEM((rows, width), bf16)
    gated = pltpu.VMEM((rows, chans), bf16)
    own, other, *sent = call(
        functools.partial(gate_kernel, found),
        "gate",
        [gated] * 2 + [block] * early,
        [VMEM] * 7,
        cost_estimate=pl.CostEstimate(flops=4 * 10**9, bytes_accessed=16 * 2**20, transcendentals=0),
    )(turned, query, early_weight, *pieces)
    last, partner = call(
        functools.partial(near_kernel, found, early), "near", [block] * 2, [VMEM] * 7
    )(own, other, late_weight, *pieces)
    operator_out, kept = call(
        keep_kernel,
        "keep",
        [jax.ShapeDtypeStruct((rows, chans), bf16), pltpu.VMEM((rows, width), f32)],
        [VMEM, ANY],
        [pltpu.VMEM((chans, width), bf16), dma((1,))],
    )(own, out_weight)
    parts = [kept]
    for part, step in zip((*sent, last), steps, strict=True):
        pairs = [(i, (i + (step if i % PAIR else planes - step)) % planes) for i in range(planes)]
        parts.append(lax.ppermute(part, chan, pairs))
    parts.append(lax.ppermute(partner, "side", swap))
    (projected,) = call(sum_kernel, "sum", [jax.ShapeDtypeStruct((rows, width), bf16)], [VMEM] * len(parts))(*parts)
    return (operator_out, projected)


def solution(mesh):
    seq_count, chan_count = mesh.shape["seq"], mesh.shape["chan"]
    shape = (seq_count // 2, 2, chan_count // PAIR, PAIR)
    paired = Mesh(mesh.devices.reshape(shape), ("zx", "core", "quad", "side"))
    seq, chan = ("zx", "core"), ("quad", "side")
    placed = (
        P(seq, chan),
        P(seq, chan),
        P(seq, chan),
        P(seq, chan),
        P(chan),
        P(chan, None),
    )
    return jax.shard_map(
        shards,
        mesh=paired,
        in_specs=placed,
        out_specs=(P(seq, chan), P(seq, chan)),
        check_vma=False,
    )
```

```python
import functools

import jax
import jax.numpy as jnp
import numpy as np
from jax import lax
from jax.experimental import pallas as pl
from jax.experimental.pallas import tpu as pltpu
from jax.sharding import Mesh
from jax.sharding import PartitionSpec as P

f32 = jnp.float32
bf16 = jnp.bfloat16


def split(values, parts):
    pieces = []
    rest = np.asarray(values, np.float64)
    for _ in range(parts):
        piece = rest.astype(bf16)
        pieces.append(piece)
        rest = rest - piece.astype(np.float64)
    return pieces


def transform_tables(order, inner):
    outer = len(order)
    length = outer * inner
    row = np.arange(outer, dtype=np.float64)
    block = np.asarray(order, np.float64)
    lane = np.arange(inner, dtype=np.float64)
    angle = 2.0 * np.pi * np.outer(row + 0.25, block) / outer
    first = np.concatenate([np.cos(angle), -np.sin(angle)], axis=0)
    twist = 2.0 * np.pi * np.outer(row + 0.25, lane) / length
    angle = 2.0 * np.pi * np.outer(lane, lane) / inner
    cos, sin = np.cos(angle), np.sin(angle)
    second = np.block([[cos, -sin], [sin, cos]])
    angle = 2.0 * np.pi * np.outer(block, row + 0.25) / outer
    last = np.concatenate([np.cos(angle), -np.sin(angle)], axis=1) / length
    first_parts = np.concatenate(split(first, 3), axis=1)
    second_parts = split(second, 2)
    back_parts = split(second.T, 2)
    last_high, last_low = split(last, 2)
    last_parts = np.concatenate([last_high, last_low, last_high], axis=1)
    return (
        first_parts,
        np.cos(twist).astype(np.float32),
        np.sin(twist).astype(np.float32),
        second_parts[0],
        second_parts[1],
        back_parts[0],
        back_parts[1],
        last_parts,
    )


def dot(a, b):
    return jnp.dot(a, b, preferred_element_type=f32)


def halves(values):
    high = values.astype(bf16)
    return high, (values - high.astype(f32)).astype(bf16)


PAIR = 2
FIRST = (6, 2)


def served(plane, step, planes):
    return lax.rem(plane + planes + step * (PAIR * lax.rem(plane, PAIR) - 1), planes)


def ranked():
    z, x, core = np.meshgrid(np.arange(8), np.arange(4), np.arange(2), indexing="ij")
    return [int(i) for i in (((z + FIRST[0]) % 8 * 4 + (x + FIRST[1]) % 4) * 2 + core).reshape(-1)]


def rank():
    zx = lax.axis_index("zx")
    z, x = lax.rem(zx // 4 + 8 - FIRST[0], 8), lax.rem(lax.rem(zx, 4) + 4 - FIRST[1], 4)
    return (z * 4 + x) * 2 + lax.axis_index("core")


def place():
    plane = PAIR * lax.axis_index("quad") + lax.axis_index("side")
    return plane, plane + 1 - PAIR * lax.axis_index("side")


def columns_of(plane, width):
    return pl.ds(pl.multiple_of(plane * width, width), width)


def fetch(pairs, sems):
    copies = [pltpu.make_async_copy(src, dst, sems.at[i]) for i, (src, dst) in enumerate(pairs)]
    for copy in copies:
        copy.start()
    return copies


def wait_all(copies):
    for copy in copies:
        copy.wait()


def pack_kernel(shares, key_ref, value_ref, filter_ref, out_ref, held, sems):
    rows, chans = key_ref.shape
    group = chans // shares
    wait_all(fetch([(ref, held.at[i]) for i, ref in enumerate((key_ref, value_ref, filter_ref))], sems))
    products = (held[0].astype(f32) * held[1].astype(f32)).astype(bf16).astype(f32)
    turned = [piece.T.reshape(shares, group, rows) for piece in (products, held[2].astype(f32))]
    out_ref[...] = jnp.concatenate(turned, axis=1).reshape(out_ref.shape).astype(bf16)


def convolve_kernel(
    group,
    outer,
    skip,
    packed,
    first_ref,
    cos_ref,
    sin_ref,
    second_high,
    second_low,
    back_high,
    back_low,
    last_ref,
    out_ref,
    wide,
    turned,
):
    inner = packed.shape[1]
    signals = 2 * group
    step = 2 * group
    wide[...] = packed[...].astype(f32)
    cos, sin = cos_ref[...], sin_ref[...]
    taken = [wide[pl.ds(i, outer, stride=step), :] for i in range(signals)]
    stacked = jnp.concatenate([t.astype(bf16) for t in taken], axis=1)
    front = dot(first_ref[...], jnp.concatenate([stacked] * 3, axis=0))
    rows = []
    for i in range(signals):
        re = front[:outer, i * inner : (i + 1) * inner]
        im = front[outer:, i * inner : (i + 1) * inner]
        rows.append(jnp.concatenate([re * cos + im * sin, im * cos - re * sin], axis=1))
    high, low = halves(jnp.concatenate(rows, axis=0))
    spec = dot(high, second_high[...]) + dot(low, second_high[...]) + dot(high, second_low[...])
    half = group * outer
    a_re, a_im = spec[:half, :inner], spec[:half, inner:]
    b_re, b_im = spec[half:, :inner], spec[half:, inner:]
    prod = jnp.concatenate([a_re * b_re - a_im * b_im, a_re * b_im + a_im * b_re], axis=1)
    high, low = halves(prod)
    back = dot(high, back_high[...]) + dot(low, back_high[...]) + dot(high, back_low[...])
    columns = []
    for i in range(group):
        re = back[i * outer : (i + 1) * outer, :inner]
        im = back[i * outer : (i + 1) * outer, inner:]
        columns.append(jnp.concatenate([re * cos - im * sin, re * sin + im * cos], axis=0))
    high, low = halves(jnp.concatenate(columns, axis=1))
    result = dot(last_ref[...], jnp.concatenate([high, high, low], axis=0))
    base = rank() * group
    for i in range(group):
        summed = result[:, i * inner : (i + 1) * inner] + skip[base + i] * taken[i]
        turned[pl.ds(i, outer, stride=group), :] = summed
    out = turned[...].astype(bf16)
    for i in range(PAIR):
        out_ref[i] = out


def segments(steps, half, rows):
    middle = len(steps) // 2
    found, at = [], [0, 0]

    def put(piece, index, row, count):
        found.append((piece, at[piece], index, row, count))
        at[piece] += count

    for index in range(middle):
        put(0, index, 0, half)
    put(0, middle, 0, half // 2)
    put(1, middle, half // 2, half // 2)
    for index in range(middle + 1, len(steps)):
        put(1, index, 0, half)
    for piece in range(2):
        put(piece, len(steps), piece * rows // 2, rows // 2)
    return at[0], found


def ship_kernel(steps, planes, found, query_ref, weight_ref, packed_ref, *rest):
    del packed_ref
    *out_refs, sems = rest
    partner = place()[1]
    width = out_refs[0].shape[1]
    base = lax.axis_index("core") * (weight_ref.shape[0] // 2)
    pairs = []
    for piece, at, index, row, count in found:
        if index < len(steps):
            rows = pl.ds(pl.multiple_of(base + row, 16), count)
            source = weight_ref.at[rows, columns_of(served(partner, steps[index], planes), width)]
        else:
            source = query_ref.at[pl.ds(row, count)]
        pairs.append((source, out_refs[piece].at[pl.ds(at, count)]))
    wait_all(fetch(pairs, sems))


def hold_kernel(*refs):
    del refs


def stage_kernel(steps, planes, query_ref, weight_ref, after_ref, early_ref, query_out, late_ref, sems):
    del after_ref
    plane, partner = place()
    width = early_ref.shape[2]
    early = early_ref.shape[0]
    targets = [served(plane, step, planes) for step in steps] + [partner]
    pairs = [(query_ref, query_out)]
    for i, target in enumerate(targets):
        held = early_ref.at[i] if i < early else late_ref.at[i - early]
        pairs.append((weight_ref.at[:, columns_of(target, width)], held))
    wait_all(fetch(pairs, sems))


def across(found, index, other, near_refs, far_refs):
    half = other.shape[1] // 2
    low, high = other[:, :half], other[:, half:]
    first = lax.axis_index("core") == 0
    near, far = jnp.where(first, low, high), jnp.where(first, high, low)
    total = None
    for piece, at, owner, row, count in found:
        if owner == index:
            rows = pl.ds(at, count)
            part = dot(near[:, row : row + count], near_refs[piece][rows, :])
            part = part + dot(far[:, row : row + count], far_refs[piece][rows, :])
            total = part if total is None else total + part
    return total


def gate_kernel(found, turned_ref, query_ref, early_ref, *rest):
    near_refs, far_refs, (own_ref, other_ref, *partial_refs) = rest[:2], rest[2:4], rest[4:]
    side = lax.axis_index("side")
    count = max(index for _, _, index, _, _ in found)
    passed = [near_refs[piece][pl.ds(at, size), :] for piece, at, index, _, size in found if index == count]
    passed = jnp.concatenate(passed, axis=0)
    other = (passed.astype(f32) * turned_ref[1 - side].astype(f32).T).astype(bf16)
    own = (query_ref[...].astype(f32) * turned_ref[side].astype(f32).T).astype(bf16)
    own_ref[...] = own
    other_ref[...] = other
    for i, partial_ref in enumerate(partial_refs):
        partial_ref[...] = (dot(own, early_ref[i]) + across(found, i, other, near_refs, far_refs)).astype(bf16)


def near_kernel(found, index, own_ref, other_ref, late_ref, *rest):
    near_refs, far_refs, (served_ref, partner_ref) = rest[:2], rest[2:4], rest[4:]
    own = own_ref[...]
    served_ref[...] = (dot(own, late_ref[0]) + across(found, index, other_ref[...], near_refs, far_refs)).astype(bf16)
    partner_ref[...] = dot(own, late_ref[1]).astype(bf16)


def keep_kernel(own_ref, weight_ref, out_ref, kept_ref, held, sems):
    copies = fetch([(weight_ref.at[:, columns_of(place()[0], held.shape[1])], held)], sems)
    own = own_ref[...]
    out_ref[...] = own
    wait_all(copies)
    kept_ref[...] = dot(own, held[...])


def sum_kernel(*refs):
    *parts, out_ref = refs
    total = parts[0][...]
    for part in parts[1:]:
        total = total + part[...].astype(f32)
    out_ref[...] = total.astype(out_ref.dtype)


ANY = pl.BlockSpec(memory_space=pl.ANY)
VMEM = pl.BlockSpec(memory_space=pltpu.VMEM)
SMEM = pl.BlockSpec(memory_space=pltpu.SMEM)
params = pltpu.CompilerParams(vmem_limit_bytes=32 * 1024 * 1024)
dma = pltpu.SemaphoreType.DMA


def call(kernel, name, out_shape, in_specs, scratch=(), **options):
    options.setdefault("out_specs", [VMEM] * len(out_shape))
    return pl.pallas_call(
        kernel,
        out_shape=out_shape,
        in_specs=in_specs,
        scratch_shapes=list(scratch),
        compiler_params=params,
        name=name,
        **options,
    )


def in_vmem(*arrays):
    return [pltpu.with_memory_space_constraint(x, pltpu.VMEM) for x in arrays]


def permuted_after(array, after, axis, pairs):
    (array,) = call(
        hold_kernel,
        "hold",
        [jax.ShapeDtypeStruct(array.shape, array.dtype)],
        [ANY] * 2,
        out_specs=[ANY],
        input_output_aliases={0: 0},
    )(array, after)
    return array, lax.ppermute(array, axis, pairs)


def shards(key_branch, value_branch, query_branch, long_filter, skip_scale, out_weight):
    seq, chan = ("zx", "core"), ("quad", "side")
    seq_count = lax.axis_size("zx") * lax.axis_size("core")
    planes = PAIR * lax.axis_size("quad")
    steps = (2, 3, 1)
    assert planes == PAIR * (len(steps) + 1)
    rows, chans = key_branch.shape
    group = chans // seq_count
    width = out_weight.shape[1] // planes
    order = ranked()
    assert sorted(order) == list(range(seq_count))
    tables = transform_tables(order, rows)
    key_branch, value_branch, query_branch, long_filter, out_weight = [
        pltpu.with_memory_space_constraint(x, pltpu.HBM)
        for x in (key_branch, value_branch, query_branch, long_filter, out_weight)
    ]
    (packed,) = call(
        functools.partial(pack_kernel, seq_count),
        "pack",
        [pltpu.VMEM((2 * chans, rows), bf16)],
        [ANY] * 3,
        [pltpu.VMEM((3, rows, chans), bf16), dma((3,))],
    )(key_branch, value_branch, long_filter)
    arrived = lax.all_to_all(
        packed.reshape(seq_count, 2 * group, rows),
        seq,
        split_axis=0,
        concat_axis=0,
        axis_index_groups=[order],
        tiled=True,
    ).reshape(2 * chans, rows)
    swap = [(0, 1), (1, 0)]
    size, found = segments(steps, chans // 2, rows)
    near = call(
        functools.partial(ship_kernel, steps, planes, found),
        "ship",
        [pltpu.VMEM((size, width), bf16)] * 2,
        [ANY] * 3,
        [dma((len(found),))],
    )(query_branch, out_weight, packed)
    near = [lax.ppermute(x, "side", swap) for x in near]
    (turned,) = call(
        functools.partial(convolve_kernel, group, seq_count),
        "convolve",
        [pltpu.VMEM((PAIR, chans, rows), bf16)],
        [SMEM] + [VMEM] * (1 + len(tables)),
        [pltpu.VMEM((2 * chans, rows), f32), pltpu.VMEM((chans, rows), f32)],
    )(skip_scale, arrived, *[jnp.asarray(t) for t in tables])
    near, far = zip(*[permuted_after(x, turned, "core", swap) for x in near], strict=True)
    early = len(steps) - 1
    early_weight, query, late_weight = call(
        functools.partial(stage_kernel, steps, planes),
        "stage",
        [
            pltpu.VMEM((early, chans, width), bf16),
            pltpu.VMEM((rows, chans), bf16),
            pltpu.HBM((2, chans, width), bf16),
        ],
        [ANY] * 3,
        [dma((len(steps) + 2,))],
    )(query_branch, out_weight, turned)
    early_weight, query = in_vmem(early_weight, query)
    pieces = in_vmem(*near, *far)
    turned = lax.all_to_all(
        turned.reshape(PAIR * seq_count, group, rows),
        ("side",) + seq,
        split_axis=0,
        concat_axis=0,
        axis_index_groups=[[side * seq_count + i for side in range(PAIR) for i in order]],
        tiled=True,
    ).reshape(PAIR, chans, rows)
    block = pltpu.VMEM((rows, width), bf16)
    gated = pltpu.VMEM((rows, chans), bf16)
    own, other, *sent = call(
        functools.partial(gate_kernel, found),
        "gate",
        [gated] * 2 + [block] * early,
        [VMEM] * 7,
        cost_estimate=pl.CostEstimate(flops=4 * 10**9, bytes_accessed=16 * 2**20, transcendentals=0),
    )(turned, query, early_weight, *pieces)
    last, partner = call(
        functools.partial(near_kernel, found, early), "near", [block] * 2, [VMEM] * 7
    )(own, other, late_weight, *pieces)
    operator_out, kept = call(
        keep_kernel,
        "keep",
        [jax.ShapeDtypeStruct((rows, chans), bf16), pltpu.VMEM((rows, width), f32)],
        [VMEM, ANY],
        [pltpu.VMEM((chans, width), bf16), dma((1,))],
    )(own, out_weight)
    parts = [kept]
    for part, step in zip((*sent, last), steps, strict=True):
        pairs = [(i, (i + (step if i % PAIR else planes - step)) % planes) for i in range(planes)]
        parts.append(lax.ppermute(part, chan, pairs))
    parts.append(lax.ppermute(partner, "side", swap))
    (projected,) = call(sum_kernel, "sum", [jax.ShapeDtypeStruct((rows, width), bf16)], [VMEM] * len(parts))(*parts)
    return (operator_out, projected)


def solution(mesh):
    seq_count, chan_count = mesh.shape["seq"], mesh.shape["chan"]
    shape = (seq_count // 2, 2, chan_count // PAIR, PAIR)
    paired = Mesh(mesh.devices.reshape(shape), ("zx", "core", "quad", "side"))
    seq, chan = ("zx", "core"), ("quad", "side")
    placed = (
        P(seq, chan),
        P(seq, chan),
        P(seq, chan),
        P(seq, chan),
        P(chan),
        P(chan, None),
    )
    return jax.shard_map(
        shards,
        mesh=paired,
        in_specs=placed,
        out_specs=(P(seq, chan), P(seq, chan)),
        check_vma=False,
    )
```

```python
import functools

import jax
import jax.numpy as jnp
import numpy as np
from jax import lax
from jax.experimental import pallas as pl
from jax.experimental.pallas import tpu as pltpu
from jax.sharding import Mesh
from jax.sharding import PartitionSpec as P

f32 = jnp.float32
bf16 = jnp.bfloat16


def split(values, parts):
    pieces = []
    rest = np.asarray(values, np.float64)
    for _ in range(parts):
        piece = rest.astype(bf16)
        pieces.append(piece)
        rest = rest - piece.astype(np.float64)
    return pieces


def transform_tables(order, inner):
    outer = len(order)
    length = outer * inner
    row = np.arange(outer, dtype=np.float64)
    block = np.asarray(order, np.float64)
    lane = np.arange(inner, dtype=np.float64)
    angle = 2.0 * np.pi * np.outer(row + 0.25, block) / outer
    first = np.concatenate([np.cos(angle), -np.sin(angle)], axis=0)
    twist = 2.0 * np.pi * np.outer(row + 0.25, lane) / length
    angle = 2.0 * np.pi * np.outer(lane, lane) / inner
    cos, sin = np.cos(angle), np.sin(angle)
    second = np.block([[cos, -sin], [sin, cos]])
    angle = 2.0 * np.pi * np.outer(block, row + 0.25) / outer
    last = np.concatenate([np.cos(angle), -np.sin(angle)], axis=1) / length
    first_parts = np.concatenate(split(first, 3), axis=1)
    second_parts = split(second, 2)
    back_parts = split(second.T, 2)
    last_high, last_low = split(last, 2)
    last_parts = np.concatenate([last_high, last_low, last_high], axis=1)
    return (
        first_parts,
        np.cos(twist).astype(np.float32),
        np.sin(twist).astype(np.float32),
        second_parts[0],
        second_parts[1],
        back_parts[0],
        back_parts[1],
        last_parts,
    )


def dot(a, b):
    return jnp.dot(a, b, preferred_element_type=f32)


def halves(values):
    high = values.astype(bf16)
    return high, (values - high.astype(f32)).astype(bf16)


PAIR = 2
FIRST = (6, 3)


def served(plane, step, planes):
    return lax.rem(plane + planes + step * (PAIR * lax.rem(plane, PAIR) - 1), planes)


def ranked():
    z, x, core = np.meshgrid(np.arange(8), np.arange(4), np.arange(2), indexing="ij")
    return [int(i) for i in (((z + FIRST[0]) % 8 * 4 + (x + FIRST[1]) % 4) * 2 + 1 - core).reshape(-1)]


def rank():
    zx = lax.axis_index("zx")
    z, x = lax.rem(zx // 4 + 8 - FIRST[0], 8), lax.rem(lax.rem(zx, 4) + 4 - FIRST[1], 4)
    return (z * 4 + x) * 2 + 1 - lax.axis_index("core")


def place():
    plane = PAIR * lax.axis_index("quad") + lax.axis_index("side")
    return plane, plane + 1 - PAIR * lax.axis_index("side")


def columns_of(plane, width):
    return pl.ds(pl.multiple_of(plane * width, width), width)


def fetch(pairs, sems):
    copies = [pltpu.make_async_copy(src, dst, sems.at[i]) for i, (src, dst) in enumerate(pairs)]
    for copy in copies:
        copy.start()
    return copies


def wait_all(copies):
    for copy in copies:
        copy.wait()


def pack_kernel(shares, key_ref, value_ref, filter_ref, out_ref, held, sems):
    rows, chans = key_ref.shape
    group = chans // shares
    wait_all(fetch([(ref, held.at[i]) for i, ref in enumerate((key_ref, value_ref, filter_ref))], sems))
    products = (held[0].astype(f32) * held[1].astype(f32)).astype(bf16).astype(f32)
    turned = [piece.T.reshape(shares, group, rows) for piece in (products, held[2].astype(f32))]
    out_ref[...] = jnp.concatenate(turned, axis=1).reshape(out_ref.shape).astype(bf16)


def convolve_kernel(
    group,
    outer,
    skip,
    packed,
    first_ref,
    cos_ref,
    sin_ref,
    second_high,
    second_low,
    back_high,
    back_low,
    last_ref,
    out_ref,
    wide,
    turned,
):
    inner = packed.shape[1]
    signals = 2 * group
    step = 2 * group
    wide[...] = packed[...].astype(f32)
    cos, sin = cos_ref[...], sin_ref[...]
    taken = [wide[pl.ds(i, outer, stride=step), :] for i in range(signals)]
    stacked = jnp.concatenate([t.astype(bf16) for t in taken], axis=1)
    front = dot(first_ref[...], jnp.concatenate([stacked] * 3, axis=0))
    rows = []
    for i in range(signals):
        re = front[:outer, i * inner : (i + 1) * inner]
        im = front[outer:, i * inner : (i + 1) * inner]
        rows.append(jnp.concatenate([re * cos + im * sin, im * cos - re * sin], axis=1))
    high, low = halves(jnp.concatenate(rows, axis=0))
    spec = dot(high, second_high[...]) + dot(low, second_high[...]) + dot(high, second_low[...])
    half = group * outer
    a_re, a_im = spec[:half, :inner], spec[:half, inner:]
    b_re, b_im = spec[half:, :inner], spec[half:, inner:]
    prod = jnp.concatenate([a_re * b_re - a_im * b_im, a_re * b_im + a_im * b_re], axis=1)
    high, low = halves(prod)
    back = dot(high, back_high[...]) + dot(low, back_high[...]) + dot(high, back_low[...])
    columns = []
    for i in range(group):
        re = back[i * outer : (i + 1) * outer, :inner]
        im = back[i * outer : (i + 1) * outer, inner:]
        columns.append(jnp.concatenate([re * cos - im * sin, re * sin + im * cos], axis=0))
    high, low = halves(jnp.concatenate(columns, axis=1))
    result = dot(last_ref[...], jnp.concatenate([high, high, low], axis=0))
    base = rank() * group
    for i in range(group):
        summed = result[:, i * inner : (i + 1) * inner] + skip[base + i] * taken[i]
        turned[pl.ds(i, outer, stride=group), :] = summed
    out = turned[...].astype(bf16)
    for i in range(PAIR):
        out_ref[i] = out


def segments(steps, half, rows):
    middle = len(steps) // 2
    found, at = [], [0, 0]

    def put(piece, index, row, count):
        found.append((piece, at[piece], index, row, count))
        at[piece] += count

    for index in range(middle):
        put(0, index, 0, half)
    put(0, middle, 0, half // 2)
    put(1, middle, half // 2, half // 2)
    for index in range(middle + 1, len(steps)):
        put(1, index, 0, half)
    for piece in range(2):
        put(piece, len(steps), piece * rows // 2, rows // 2)
    return at[0], found


def ship_kernel(steps, planes, found, query_ref, weight_ref, packed_ref, *rest):
    del packed_ref
    *out_refs, sems = rest
    partner = place()[1]
    width = out_refs[0].shape[1]
    base = lax.axis_index("core") * (weight_ref.shape[0] // 2)
    pairs = []
    for piece, at, index, row, count in found:
        if index < len(steps):
            rows = pl.ds(pl.multiple_of(base + row, 16), count)
            source = weight_ref.at[rows, columns_of(served(partner, steps[index], planes), width)]
        else:
            source = query_ref.at[pl.ds(row, count)]
        pairs.append((source, out_refs[piece].at[pl.ds(at, count)]))
    wait_all(fetch(pairs, sems))


def hold_kernel(*refs):
    del refs


def stage_kernel(steps, planes, query_ref, weight_ref, after_ref, early_ref, query_out, late_ref, sems):
    del after_ref
    plane, partner = place()
    width = early_ref.shape[2]
    early = early_ref.shape[0]
    targets = [served(plane, step, planes) for step in steps] + [partner]
    pairs = [(query_ref, query_out)]
    for i, target in enumerate(targets):
        held = early_ref.at[i] if i < early else late_ref.at[i - early]
        pairs.append((weight_ref.at[:, columns_of(target, width)], held))
    wait_all(fetch(pairs, sems))


def across(found, index, other, near_refs, far_refs):
    half = other.shape[1] // 2
    low, high = other[:, :half], other[:, half:]
    first = lax.axis_index("core") == 0
    near, far = jnp.where(first, low, high), jnp.where(first, high, low)
    total = None
    for piece, at, owner, row, count in found:
        if owner == index:
            rows = pl.ds(at, count)
            part = dot(near[:, row : row + count], near_refs[piece][rows, :])
            part = part + dot(far[:, row : row + count], far_refs[piece][rows, :])
            total = part if total is None else total + part
    return total


def gate_kernel(found, turned_ref, query_ref, early_ref, *rest):
    near_refs, far_refs, (own_ref, other_ref, *partial_refs) = rest[:2], rest[2:4], rest[4:]
    side = lax.axis_index("side")
    count = max(index for _, _, index, _, _ in found)
    passed = [near_refs[piece][pl.ds(at, size), :] for piece, at, index, _, size in found if index == count]
    passed = jnp.concatenate(passed, axis=0)
    other = (passed.astype(f32) * turned_ref[1 - side].astype(f32).T).astype(bf16)
    own = (query_ref[...].astype(f32) * turned_ref[side].astype(f32).T).astype(bf16)
    own_ref[...] = own
    other_ref[...] = other
    for i, partial_ref in enumerate(partial_refs):
        partial_ref[...] = (dot(own, early_ref[i]) + across(found, i, other, near_refs, far_refs)).astype(bf16)


def near_kernel(found, index, own_ref, other_ref, late_ref, *rest):
    near_refs, far_refs, (served_ref, partner_ref) = rest[:2], rest[2:4], rest[4:]
    own = own_ref[...]
    served_ref[...] = (dot(own, late_ref[0]) + across(found, index, other_ref[...], near_refs, far_refs)).astype(bf16)
    partner_ref[...] = dot(own, late_ref[1]).astype(bf16)


def keep_kernel(own_ref, weight_ref, out_ref, kept_ref, held, sems):
    copies = fetch([(weight_ref.at[:, columns_of(place()[0], held.shape[1])], held)], sems)
    own = own_ref[...]
    out_ref[...] = own
    wait_all(copies)
    kept_ref[...] = dot(own, held[...])


def sum_kernel(*refs):
    *parts, out_ref = refs
    total = parts[0][...]
    for part in parts[1:]:
        total = total + part[...].astype(f32)
    out_ref[...] = total.astype(out_ref.dtype)


ANY = pl.BlockSpec(memory_space=pl.ANY)
VMEM = pl.BlockSpec(memory_space=pltpu.VMEM)
SMEM = pl.BlockSpec(memory_space=pltpu.SMEM)
params = pltpu.CompilerParams(vmem_limit_bytes=32 * 1024 * 1024)
dma = pltpu.SemaphoreType.DMA


def call(kernel, name, out_shape, in_specs, scratch=(), **options):
    options.setdefault("out_specs", [VMEM] * len(out_shape))
    return pl.pallas_call(
        kernel,
        out_shape=out_shape,
        in_specs=in_specs,
        scratch_shapes=list(scratch),
        compiler_params=params,
        name=name,
        **options,
    )


def in_vmem(*arrays):
    return [pltpu.with_memory_space_constraint(x, pltpu.VMEM) for x in arrays]


def permuted_after(array, after, axis, pairs):
    (array,) = call(
        hold_kernel,
        "hold",
        [jax.ShapeDtypeStruct(array.shape, array.dtype)],
        [ANY] * 2,
        out_specs=[ANY],
        input_output_aliases={0: 0},
    )(array, after)
    return array, lax.ppermute(array, axis, pairs)


def shards(key_branch, value_branch, query_branch, long_filter, skip_scale, out_weight):
    seq, chan = ("zx", "core"), ("quad", "side")
    seq_count = lax.axis_size("zx") * lax.axis_size("core")
    planes = PAIR * lax.axis_size("quad")
    steps = (2, 3, 1)
    assert planes == PAIR * (len(steps) + 1)
    rows, chans = key_branch.shape
    group = chans // seq_count
    width = out_weight.shape[1] // planes
    order = ranked()
    assert sorted(order) == list(range(seq_count))
    tables = transform_tables(order, rows)
    key_branch, value_branch, query_branch, long_filter, out_weight = [
        pltpu.with_memory_space_constraint(x, pltpu.HBM)
        for x in (key_branch, value_branch, query_branch, long_filter, out_weight)
    ]
    (packed,) = call(
        functools.partial(pack_kernel, seq_count),
        "pack",
        [pltpu.VMEM((2 * chans, rows), bf16)],
        [ANY] * 3,
        [pltpu.VMEM((3, rows, chans), bf16), dma((3,))],
    )(key_branch, value_branch, long_filter)
    arrived = lax.all_to_all(
        packed.reshape(seq_count, 2 * group, rows),
        seq,
        split_axis=0,
        concat_axis=0,
        axis_index_groups=[order],
        tiled=True,
    ).reshape(2 * chans, rows)
    swap = [(0, 1), (1, 0)]
    size, found = segments(steps, chans // 2, rows)
    near = call(
        functools.partial(ship_kernel, steps, planes, found),
        "ship",
        [pltpu.VMEM((size, width), bf16)] * 2,
        [ANY] * 3,
        [dma((len(found),))],
    )(query_branch, out_weight, packed)
    near = [lax.ppermute(x, "side", swap) for x in near]
    (turned,) = call(
        functools.partial(convolve_kernel, group, seq_count),
        "convolve",
        [pltpu.VMEM((PAIR, chans, rows), bf16)],
        [SMEM] + [VMEM] * (1 + len(tables)),
        [pltpu.VMEM((2 * chans, rows), f32), pltpu.VMEM((chans, rows), f32)],
    )(skip_scale, arrived, *[jnp.asarray(t) for t in tables])
    near, far = zip(*[permuted_after(x, turned, "core", swap) for x in near], strict=True)
    early = len(steps) - 1
    early_weight, query, late_weight = call(
        functools.partial(stage_kernel, steps, planes),
        "stage",
        [
            pltpu.VMEM((early, chans, width), bf16),
            pltpu.VMEM((rows, chans), bf16),
            pltpu.HBM((2, chans, width), bf16),
        ],
        [ANY] * 3,
        [dma((len(steps) + 2,))],
    )(query_branch, out_weight, turned)
    early_weight, query = in_vmem(early_weight, query)
    pieces = in_vmem(*near, *far)
    turned = lax.all_to_all(
        turned.reshape(PAIR * seq_count, group, rows),
        ("side",) + seq,
        split_axis=0,
        concat_axis=0,
        axis_index_groups=[[side * seq_count + i for side in range(PAIR) for i in order]],
        tiled=True,
    ).reshape(PAIR, chans, rows)
    block = pltpu.VMEM((rows, width), bf16)
    gated = pltpu.VMEM((rows, chans), bf16)
    own, other, *sent = call(
        functools.partial(gate_kernel, found),
        "gate",
        [gated] * 2 + [block] * early,
        [VMEM] * 7,
        cost_estimate=pl.CostEstimate(flops=4 * 10**9, bytes_accessed=16 * 2**20, transcendentals=0),
    )(turned, query, early_weight, *pieces)
    last, partner = call(
        functools.partial(near_kernel, found, early), "near", [block] * 2, [VMEM] * 7
    )(own, other, late_weight, *pieces)
    operator_out, kept = call(
        keep_kernel,
        "keep",
        [jax.ShapeDtypeStruct((rows, chans), bf16), pltpu.VMEM((rows, width), f32)],
        [VMEM, ANY],
        [pltpu.VMEM((chans, width), bf16), dma((1,))],
    )(own, out_weight)
    parts = [kept]
    for part, step in zip((*sent, last), steps, strict=True):
        pairs = [(i, (i + (step if i % PAIR else planes - step)) % planes) for i in range(planes)]
        parts.append(lax.ppermute(part, chan, pairs))
    parts.append(lax.ppermute(partner, "side", swap))
    (projected,) = call(sum_kernel, "sum", [jax.ShapeDtypeStruct((rows, width), bf16)], [VMEM] * len(parts))(*parts)
    return (operator_out, projected)


def solution(mesh):
    seq_count, chan_count = mesh.shape["seq"], mesh.shape["chan"]
    shape = (seq_count // 2, 2, chan_count // PAIR, PAIR)
    paired = Mesh(mesh.devices.reshape(shape), ("zx", "core", "quad", "side"))
    seq, chan = ("zx", "core"), ("quad", "side")
    placed = (
        P(seq, chan),
        P(seq, chan),
        P(seq, chan),
        P(seq, chan),
        P(chan),
        P(chan, None),
    )
    return jax.shard_map(
        shards,
        mesh=paired,
        in_specs=placed,
        out_specs=(P(seq, chan), P(seq, chan)),
        check_vma=False,
    )
```

```python
import functools

import jax
import jax.numpy as jnp
import numpy as np
from jax import lax
from jax.experimental import pallas as pl
from jax.experimental.pallas import tpu as pltpu
from jax.sharding import Mesh
from jax.sharding import PartitionSpec as P

f32 = jnp.float32
bf16 = jnp.bfloat16


def split(values, parts):
    pieces = []
    rest = np.asarray(values, np.float64)
    for _ in range(parts):
        piece = rest.astype(bf16)
        pieces.append(piece)
        rest = rest - piece.astype(np.float64)
    return pieces


def transform_tables(order, inner):
    outer = len(order)
    length = outer * inner
    row = np.arange(outer, dtype=np.float64)
    block = np.asarray(order, np.float64)
    lane = np.arange(inner, dtype=np.float64)
    angle = 2.0 * np.pi * np.outer(row + 0.25, block) / outer
    first = np.concatenate([np.cos(angle), -np.sin(angle)], axis=0)
    twist = 2.0 * np.pi * np.outer(row + 0.25, lane) / length
    angle = 2.0 * np.pi * np.outer(lane, lane) / inner
    cos, sin = np.cos(angle), np.sin(angle)
    second = np.block([[cos, -sin], [sin, cos]])
    angle = 2.0 * np.pi * np.outer(block, row + 0.25) / outer
    last = np.concatenate([np.cos(angle), -np.sin(angle)], axis=1) / length
    first_parts = np.concatenate(split(first, 3), axis=1)
    second_parts = split(second, 2)
    back_parts = split(second.T, 2)
    last_high, last_low = split(last, 2)
    last_parts = np.concatenate([last_high, last_low, last_high], axis=1)
    return (
        first_parts,
        np.cos(twist).astype(np.float32),
        np.sin(twist).astype(np.float32),
        second_parts[0],
        second_parts[1],
        back_parts[0],
        back_parts[1],
        last_parts,
    )


def dot(a, b):
    return jnp.dot(a, b, preferred_element_type=f32)


def halves(values):
    high = values.astype(bf16)
    return high, (values - high.astype(f32)).astype(bf16)


PAIR = 2
FIRST = (6, 3)


def served(plane, step, planes):
    return lax.rem(plane + planes + step * (PAIR * lax.rem(plane, PAIR) - 1), planes)


def ranked():
    z, x, core = np.meshgrid(np.arange(8), np.arange(4), np.arange(2), indexing="ij")
    return [int(i) for i in (((z + FIRST[0]) % 8 * 4 + (x + FIRST[1]) % 4) * 2 + 1 - core).reshape(-1)]


def rank():
    zx = lax.axis_index("zx")
    z, x = lax.rem(zx // 4 + 8 - FIRST[0], 8), lax.rem(lax.rem(zx, 4) + 4 - FIRST[1], 4)
    return (z * 4 + x) * 2 + 1 - lax.axis_index("core")


def place():
    plane = PAIR * lax.axis_index("quad") + lax.axis_index("side")
    return plane, plane + 1 - PAIR * lax.axis_index("side")


def columns_of(plane, width):
    return pl.ds(pl.multiple_of(plane * width, width), width)


def fetch(pairs, sems):
    copies = [pltpu.make_async_copy(src, dst, sems.at[i]) for i, (src, dst) in enumerate(pairs)]
    for copy in copies:
        copy.start()
    return copies


def wait_all(copies):
    for copy in copies:
        copy.wait()


def pack_kernel(shares, key_ref, value_ref, filter_ref, out_ref, held, sems):
    rows, chans = key_ref.shape
    group = chans // shares
    wait_all(fetch([(ref, held.at[i]) for i, ref in enumerate((key_ref, value_ref, filter_ref))], sems))
    products = (held[0].astype(f32) * held[1].astype(f32)).astype(bf16).astype(f32)
    turned = [piece.T.reshape(shares, group, rows) for piece in (products, held[2].astype(f32))]
    out_ref[...] = jnp.concatenate(turned, axis=1).reshape(out_ref.shape).astype(bf16)


def convolve_kernel(
    group,
    outer,
    skip,
    packed,
    first_ref,
    cos_ref,
    sin_ref,
    second_high,
    second_low,
    back_high,
    back_low,
    last_ref,
    out_ref,
    wide,
    turned,
):
    inner = packed.shape[1]
    signals = 2 * group
    step = 2 * group
    wide[...] = packed[...].astype(f32)
    cos, sin = cos_ref[...], sin_ref[...]
    taken = [wide[pl.ds(i, outer, stride=step), :] for i in range(signals)]
    stacked = jnp.concatenate([t.astype(bf16) for t in taken], axis=1)
    front = dot(first_ref[...], jnp.concatenate([stacked] * 3, axis=0))
    rows = []
    for i in range(signals):
        re = front[:outer, i * inner : (i + 1) * inner]
        im = front[outer:, i * inner : (i + 1) * inner]
        rows.append(jnp.concatenate([re * cos + im * sin, im * cos - re * sin], axis=1))
    high, low = halves(jnp.concatenate(rows, axis=0))
    spec = dot(high, second_high[...]) + dot(low, second_high[...]) + dot(high, second_low[...])
    half = group * outer
    a_re, a_im = spec[:half, :inner], spec[:half, inner:]
    b_re, b_im = spec[half:, :inner], spec[half:, inner:]
    prod = jnp.concatenate([a_re * b_re - a_im * b_im, a_re * b_im + a_im * b_re], axis=1)
    high, low = halves(prod)
    back = dot(high, back_high[...]) + dot(low, back_high[...]) + dot(high, back_low[...])
    columns = []
    for i in range(group):
        re = back[i * outer : (i + 1) * outer, :inner]
        im = back[i * outer : (i + 1) * outer, inner:]
        columns.append(jnp.concatenate([re * cos - im * sin, re * sin + im * cos], axis=0))
    high, low = halves(jnp.concatenate(columns, axis=1))
    result = dot(last_ref[...], jnp.concatenate([high, high, low], axis=0))
    base = rank() * group
    for i in range(group):
        summed = result[:, i * inner : (i + 1) * inner] + skip[base + i] * taken[i]
        turned[pl.ds(i, outer, stride=group), :] = summed
    out = turned[...].astype(bf16)
    for i in range(PAIR):
        out_ref[i] = out


def segments(steps, half, rows):
    middle = len(steps) // 2
    found, at = [], [0, 0]

    def put(piece, index, row, count):
        found.append((piece, at[piece], index, row, count))
        at[piece] += count

    for index in range(middle):
        put(0, index, 0, half)
    put(0, middle, 0, half // 2)
    put(1, middle, half // 2, half // 2)
    for index in range(middle + 1, len(steps)):
        put(1, index, 0, half)
    for piece in range(2):
        put(piece, len(steps), piece * rows // 2, rows // 2)
    return at[0], found


def ship_kernel(steps, planes, found, query_ref, weight_ref, packed_ref, *rest):
    del packed_ref
    *out_refs, sems = rest
    partner = place()[1]
    width = out_refs[0].shape[1]
    base = lax.axis_index("core") * (weight_ref.shape[0] // 2)
    pairs = []
    for piece, at, index, row, count in found:
        if index < len(steps):
            rows = pl.ds(pl.multiple_of(base + row, 16), count)
            source = weight_ref.at[rows, columns_of(served(partner, steps[index], planes), width)]
        else:
            source = query_ref.at[pl.ds(row, count)]
        pairs.append((source, out_refs[piece].at[pl.ds(at, count)]))
    wait_all(fetch(pairs, sems))


def hold_kernel(*refs):
    del refs


def stage_kernel(steps, planes, query_ref, weight_ref, after_ref, early_ref, query_out, late_ref, sems):
    del after_ref
    plane, partner = place()
    width = early_ref.shape[2]
    early = early_ref.shape[0]
    targets = [served(plane, step, planes) for step in steps] + [partner]
    pairs = [(query_ref, query_out)]
    for i, target in enumerate(targets):
        held = early_ref.at[i] if i < early else late_ref.at[i - early]
        pairs.append((weight_ref.at[:, columns_of(target, width)], held))
    wait_all(fetch(pairs, sems))


def across(found, index, other, near_refs, far_refs):
    half = other.shape[1] // 2
    low, high = other[:, :half], other[:, half:]
    first = lax.axis_index("core") == 0
    near, far = jnp.where(first, low, high), jnp.where(first, high, low)
    total = None
    for piece, at, owner, row, count in found:
        if owner == index:
            rows = pl.ds(at, count)
            part = dot(near[:, row : row + count], near_refs[piece][rows, :])
            part = part + dot(far[:, row : row + count], far_refs[piece][rows, :])
            total = part if total is None else total + part
    return total


def gate_kernel(found, turned_ref, query_ref, early_ref, *rest):
    near_refs, far_refs, (own_ref, other_ref, *partial_refs) = rest[:2], rest[2:4], rest[4:]
    side = lax.axis_index("side")
    count = max(index for _, _, index, _, _ in found)
    passed = [near_refs[piece][pl.ds(at, size), :] for piece, at, index, _, size in found if index == count]
    passed = jnp.concatenate(passed, axis=0)
    other = (passed.astype(f32) * turned_ref[side].astype(f32).T).astype(bf16)
    own = (query_ref[...].astype(f32) * turned_ref[1 - side].astype(f32).T).astype(bf16)
    own_ref[...] = own
    other_ref[...] = other
    for i, partial_ref in enumerate(partial_refs):
        partial_ref[...] = (dot(own, early_ref[i]) + across(found, i, other, near_refs, far_refs)).astype(bf16)


def near_kernel(found, index, own_ref, other_ref, late_ref, *rest):
    near_refs, far_refs, (served_ref, partner_ref) = rest[:2], rest[2:4], rest[4:]
    own = own_ref[...]
    served_ref[...] = (dot(own, late_ref[0]) + across(found, index, other_ref[...], near_refs, far_refs)).astype(bf16)
    partner_ref[...] = dot(own, late_ref[1]).astype(bf16)


def keep_kernel(own_ref, weight_ref, out_ref, kept_ref, held, sems):
    copies = fetch([(weight_ref.at[:, columns_of(place()[0], held.shape[1])], held)], sems)
    own = own_ref[...]
    out_ref[...] = own
    wait_all(copies)
    kept_ref[...] = dot(own, held[...])


def sum_kernel(*refs):
    *parts, out_ref = refs
    total = parts[0][...]
    for part in parts[1:]:
        total = total + part[...].astype(f32)
    out_ref[...] = total.astype(out_ref.dtype)


ANY = pl.BlockSpec(memory_space=pl.ANY)
VMEM = pl.BlockSpec(memory_space=pltpu.VMEM)
SMEM = pl.BlockSpec(memory_space=pltpu.SMEM)
params = pltpu.CompilerParams(vmem_limit_bytes=32 * 1024 * 1024)
dma = pltpu.SemaphoreType.DMA


def call(kernel, name, out_shape, in_specs, scratch=(), **options):
    options.setdefault("out_specs", [VMEM] * len(out_shape))
    return pl.pallas_call(
        kernel,
        out_shape=out_shape,
        in_specs=in_specs,
        scratch_shapes=list(scratch),
        compiler_params=params,
        name=name,
        **options,
    )


def in_vmem(*arrays):
    return [pltpu.with_memory_space_constraint(x, pltpu.VMEM) for x in arrays]


def permuted_after(array, after, axis, pairs):
    (array,) = call(
        hold_kernel,
        "hold",
        [jax.ShapeDtypeStruct(array.shape, array.dtype)],
        [ANY] * 2,
        out_specs=[ANY],
        input_output_aliases={0: 0},
    )(array, after)
    return array, lax.ppermute(array, axis, pairs)


def shards(key_branch, value_branch, query_branch, long_filter, skip_scale, out_weight):
    seq, chan = ("zx", "core"), ("quad", "side")
    seq_count = lax.axis_size("zx") * lax.axis_size("core")
    planes = PAIR * lax.axis_size("quad")
    steps = (2, 3, 1)
    assert planes == PAIR * (len(steps) + 1)
    rows, chans = key_branch.shape
    group = chans // seq_count
    width = out_weight.shape[1] // planes
    order = ranked()
    assert sorted(order) == list(range(seq_count))
    tables = transform_tables(order, rows)
    key_branch, value_branch, query_branch, long_filter, out_weight = [
        pltpu.with_memory_space_constraint(x, pltpu.HBM)
        for x in (key_branch, value_branch, query_branch, long_filter, out_weight)
    ]
    (packed,) = call(
        functools.partial(pack_kernel, seq_count),
        "pack",
        [pltpu.VMEM((2 * chans, rows), bf16)],
        [ANY] * 3,
        [pltpu.VMEM((3, rows, chans), bf16), dma((3,))],
    )(key_branch, value_branch, long_filter)
    arrived = lax.all_to_all(
        packed.reshape(seq_count, 2 * group, rows),
        seq,
        split_axis=0,
        concat_axis=0,
        axis_index_groups=[order],
        tiled=True,
    ).reshape(2 * chans, rows)
    swap = [(0, 1), (1, 0)]
    size, found = segments(steps, chans // 2, rows)
    near = call(
        functools.partial(ship_kernel, steps, planes, found),
        "ship",
        [pltpu.VMEM((size, width), bf16)] * 2,
        [ANY] * 3,
        [dma((len(found),))],
    )(query_branch, out_weight, packed)
    near = [lax.ppermute(x, "side", swap) for x in near]
    (turned,) = call(
        functools.partial(convolve_kernel, group, seq_count),
        "convolve",
        [pltpu.VMEM((PAIR, chans, rows), bf16)],
        [SMEM] + [VMEM] * (1 + len(tables)),
        [pltpu.VMEM((2 * chans, rows), f32), pltpu.VMEM((chans, rows), f32)],
    )(skip_scale, arrived, *[jnp.asarray(t) for t in tables])
    near, far = zip(*[permuted_after(x, turned, "core", swap) for x in near], strict=True)
    early = len(steps) - 1
    early_weight, query, late_weight = call(
        functools.partial(stage_kernel, steps, planes),
        "stage",
        [
            pltpu.VMEM((early, chans, width), bf16),
            pltpu.VMEM((rows, chans), bf16),
            pltpu.HBM((2, chans, width), bf16),
        ],
        [ANY] * 3,
        [dma((len(steps) + 2,))],
    )(query_branch, out_weight, turned)
    early_weight, query = in_vmem(early_weight, query)
    pieces = in_vmem(*near, *far)
    turned = lax.all_to_all(
        turned.reshape(PAIR * seq_count, group, rows),
        ("side",) + seq,
        split_axis=0,
        concat_axis=0,
        axis_index_groups=[[side * seq_count + i for side in (1, 0) for i in order]],
        tiled=True,
    ).reshape(PAIR, chans, rows)
    block = pltpu.VMEM((rows, width), bf16)
    gated = pltpu.VMEM((rows, chans), bf16)
    own, other, *sent = call(
        functools.partial(gate_kernel, found),
        "gate",
        [gated] * 2 + [block] * early,
        [VMEM] * 7,
        cost_estimate=pl.CostEstimate(flops=4 * 10**9, bytes_accessed=16 * 2**20, transcendentals=0),
    )(turned, query, early_weight, *pieces)
    last, partner = call(
        functools.partial(near_kernel, found, early), "near", [block] * 2, [VMEM] * 7
    )(own, other, late_weight, *pieces)
    operator_out, kept = call(
        keep_kernel,
        "keep",
        [jax.ShapeDtypeStruct((rows, chans), bf16), pltpu.VMEM((rows, width), f32)],
        [VMEM, ANY],
        [pltpu.VMEM((chans, width), bf16), dma((1,))],
    )(own, out_weight)
    parts = [kept]
    for part, step in zip((*sent, last), steps, strict=True):
        pairs = [(i, (i + (step if i % PAIR else planes - step)) % planes) for i in range(planes)]
        parts.append(lax.ppermute(part, chan, pairs))
    parts.append(lax.ppermute(partner, "side", swap))
    (projected,) = call(sum_kernel, "sum", [jax.ShapeDtypeStruct((rows, width), bf16)], [VMEM] * len(parts))(*parts)
    return (operator_out, projected)


def solution(mesh):
    seq_count, chan_count = mesh.shape["seq"], mesh.shape["chan"]
    shape = (seq_count // 2, 2, chan_count // PAIR, PAIR)
    paired = Mesh(mesh.devices.reshape(shape), ("zx", "core", "quad", "side"))
    seq, chan = ("zx", "core"), ("quad", "side")
    placed = (
        P(seq, chan),
        P(seq, chan),
        P(seq, chan),
        P(seq, chan),
        P(chan),
        P(chan, None),
    )
    return jax.shard_map(
        shards,
        mesh=paired,
        in_specs=placed,
        out_specs=(P(seq, chan), P(seq, chan)),
        check_vma=False,
    )
```
